32 devices in a mesh: py: 4 (over z), pz: 8 (over y, x, core).
Axes of the slice: x: 2, y: 2, z: 4, core: 2. Of those that a mesh axis runs over, the one named last changes fastest.
Arguments:
- conserved: float32 [5, 512, 256, 128], P(None, 'pz', 'py'), may hold values from -2 to 3.5, as said below
- register: float32 [5, 512, 256, 128], P(None, 'pz', 'py'), may hold values from -6 to 6
- stream_blocks: float32 [1, 3, 128, 128], replicated, may hold values from -0.3125 to 0.3125
- wall_matrix: float32 [256, 256], replicated, may hold values from -0.375 to 0.375
- span_blocks: float32 [16, 3, 32, 32], replicated, may hold values from -0.625 to 0.625
- inflow_gain: float32 [5], replicated, may hold values from 0.5 to 2
- source_block: int32 [32, 4096, 1], replicated, may hold values from 0 to 31; in each aligned block of 4096 rows (0 to 4095, 4096 to 8191, ..., all dimensions but the last counted through in order) at most 256 rows name the same one
- source_column: int32 [32, 4096], replicated, may hold values from 0 to 4095
Outputs:
- new_conserved: float32 [5, 512, 256, 128], P(None, 'pz', 'py')
- new_register: float32 [5, 512, 256, 128], P(None, 'pz', 'py')
The draws below stay inside these ranges and needn't reach their ends.
Inputs may be any that keep to these rules, and one draw needn't show every extreme that they name: Among the 4096 entries of one column block, source_block[b, :, 0], no value appears more than 256 times, and in some column block one value appears exactly 256 times. `conserved`: the first field, the density, lies between 0.5 and 2.
All inputs are finite; a program needn't handle non-finite values.
Results may differ from the reference program's by a relative error of at most 0.0001.
Values sent between devices are 32-bit elements; how exact they have to be, the bound alone decides.
No kernel may reach another device: no remote copies, remote signals or barrier semaphores. Data moves between devices by JAX's collectives and lax.ppermute only.
A program may use at most 192 MiB of HBM per device.

```python
import math
import jax
import jax.numpy as jnp
import numpy as np
from jax import lax

FIELDS = 5
NY = 256
NZ = 512
XBL = 128
ZBL = 32
CZ = 64
NX = 128
YROWS = 64
BLK_DEV = 4096
CAP = 256
XREC = 96
NXB = 1
NZB = 16
N_PZ = 8
DEVICES = 32


def draw_conserved(key, part):
    subkeys = jax.random.split(key, 3)
    grid_shape = (NZ, NY, NX)
    density = jax.random.uniform(subkeys[0], grid_shape, jnp.float32, 0.5, 2.0)
    momentum = 0.5 * jnp.clip(jax.random.normal(subkeys[1], (3,) + grid_shape, jnp.float32), -4.0, 4.0)
    energy = jax.random.uniform(subkeys[2], grid_shape, jnp.float32, 2.0, 3.5)
    return jnp.concatenate([density[None], momentum, energy[None]], axis=0)


def set_ends(entries, stream_key, least, top_value):
    extent = entries.shape
    place = [jax.random.randint(jax.random.fold_in(stream_key, axis), (), 0, extent[axis]) for axis in range(len(extent))]
    entries = entries.at[tuple(place)].set(least)
    longest = extent.index(max(extent))
    place[longest] = (place[longest] + 1) % extent[longest]
    return entries.at[tuple(place)].set(top_value)


def block_levels(rng, shape, cuts, low, top_value):
    def one(position, parts):
        draws = jax.random.uniform(jax.random.fold_in(jax.random.fold_in(rng, 6), position), (parts,), jnp.float32, low / len(cuts), top_value / len(cuts))
        return jnp.repeat(jnp.exp(draws), shape[position] // parts).reshape((-1,) + (1,) * (len(shape) - position - 1))

    loudness = one(*cuts[0])
    for cut in cuts[1:]:
        loudness = loudness * one(*cut)
    return loudness


def deal_out(own_key, own, number, rows, count, top, bound, lean):
    ranking = jax.random.permutation(own_key, count)
    heavy_load, usual = portions_of(count, rows * top, bound, lean, True), portions_of(count, rows * top, bound, lean, False)
    places = jnp.arange(count)

    def named(tallies, turn):
        used = int((tallies > 0).sum())
        fixed = max(1, used // 4)
        shifted = fixed + (places - fixed + turn * (used - fixed)) % max(1, count - fixed)
        return jnp.zeros((count,), jnp.int32).at[ranking[jnp.where(places < fixed, places, shifted)]].set(jnp.asarray(tallies, jnp.int32))

    tallies = jnp.where(number % 4 == 0, named(heavy_load, number // 4), named(usual, number - number // 4 - 1))
    mixed = jax.random.permutation(jax.random.fold_in(own, 3), count)
    donor, taker = mixed[0:count // 2 * 2:2], mixed[1:count // 2 * 2:2]
    margin = jnp.minimum(tallies[donor] - 1, bound - tallies[taker]) // 2
    margin = jnp.where((donor == ranking[0]) | (taker == ranking[0]) | (tallies[taker] == 0), 0, jnp.maximum(margin, 0))
    shifted = jax.random.randint(jax.random.fold_in(own, 4), (count // 2,), 0, 1 << 20) % (margin + 1)
    tallies = tallies.at[donor].add(-shifted).at[taker].add(shifted)
    items = jnp.searchsorted(jnp.cumsum(tallies), jnp.arange(rows * top), side="right").astype(jnp.int32)
    table = items.reshape(top, rows).T
    table = table[jax.random.permutation(jax.random.fold_in(own, 1), rows)]
    turn = jax.random.randint(jax.random.fold_in(own, 2), (rows, 1), 0, top)
    return jnp.take_along_axis(table, (jnp.arange(top)[None, :] + turn) % top, axis=1)


def portions_of(amount, total, reach, skew, full):
    weights = [(1 << 20) // math.isqrt(standing ** skew) + 1 for standing in range(1, amount + 1)]
    largest = reach if full else min(reach, max(-(-total // amount), total * weights[0] // sum(weights)))
    least = 1 if total - largest >= amount - 1 else 0
    holding, surplus = [largest] + [least] * (amount - 1), total - largest - least * (amount - 1)
    while surplus > 0:
        candidates = [i for i in range(1, amount) if holding[i] < largest] or [i for i in range(1, amount) if holding[i] < reach]
        whole, left = sum([weights[i] for i in candidates]), surplus
        for i in candidates:
            more = min(reach - holding[i], max(1, left * weights[i] // whole), surplus)
            holding[i] = holding[i] + more
            surplus = surplus - more
    return np.array(holding)


def bell_draw(key, extent, deviation, most, cuts=(), kind=jnp.bfloat16):
    gain = block_levels(key, extent, cuts, -0.22, 0.18) if cuts else 1.0
    result = jax.random.normal(key, extent, jnp.float32) * deviation * gain
    return jnp.minimum(jnp.maximum(result, -most), most).astype(kind)


def setup_inputs(seed: int = 0) -> dict:
    key_of = jax.random.split(jax.random.key(seed), 9)
    conserved = draw_conserved(jax.random.fold_in(key_of[8], 71), 0)
    register = bell_draw(key_of[1], (FIELDS, NZ, NY, NX), 1.0, 6.0, ((1, 8), (2, 4)), jnp.float32)
    stream_blocks = bell_draw(key_of[2], (NXB, 3, XBL, XBL), (3 * XBL) ** -0.5, 0.3125, (), jnp.float32)
    wall_matrix = bell_draw(key_of[3], (NY, NY), NY ** -0.5, 0.375, (), jnp.float32)
    span_blocks = bell_draw(key_of[4], (NZB, 3, ZBL, ZBL), (3 * ZBL) ** -0.5, 0.625, (), jnp.float32)
    inflow_gain = jnp.clip(jnp.exp(jax.random.uniform(key_of[5], (FIELDS,), jnp.float32, math.log(0.5), math.log(2.0))), 0.5, 2.0)
    source_block_keys = jax.random.split(jax.random.fold_in(key_of[6], 1), DEVICES * BLK_DEV // BLK_DEV)
    source_block_turns = jax.random.permutation(jax.random.fold_in(key_of[6], 3), DEVICES * BLK_DEV // BLK_DEV)
    source_block = jax.vmap(lambda own, number: deal_out(jax.random.fold_in(key_of[6], 2), own, number, BLK_DEV, DEVICES, 1, CAP, 2))(source_block_keys, source_block_turns).reshape((DEVICES, BLK_DEV, 1))
    source_column = set_ends(jax.random.randint(key_of[7], (DEVICES, BLK_DEV), 0, BLK_DEV), jax.random.fold_in(key_of[7], 1), 0, BLK_DEV - 1).astype(jnp.int32)
    return {"conserved": conserved, "register": register, "stream_blocks": stream_blocks, "wall_matrix": wall_matrix, "span_blocks": span_blocks, "inflow_gain": inflow_gain, "source_block": source_block, "source_column": source_column}


highest = lax.Precision.HIGHEST
section_decay = -5.0 / 9.0
section_gain = 15.0 / 16.0
time_step = 0.1


def flux_set(values, direction):
    speeds = values[1:4] / values[0]
    pressure = 0.4 * (values[4] - 0.5 * (values[1] * speeds[0] + values[2] * speeds[1] + values[3] * speeds[2]))
    velocity = speeds[direction]
    pieces = [values[1 + direction]]
    for component in range(1, 4):
        moment = values[component] * velocity
        if component - 1 == direction:
            moment = moment + pressure
        pieces.append(moment)
    pieces.append((values[4] + pressure) * velocity)
    return jnp.stack(pieces)


def stream_derivative(values, blocks):
    leading = values.shape[:-1]
    block_count = blocks.shape[0]
    block_width = blocks.shape[2]
    shaped = values.reshape(leading + (block_count, block_width))
    zero_block = jnp.zeros(leading + (1, block_width), jnp.float32)
    padded = jnp.concatenate([zero_block, shaped, zero_block], axis=-2)
    summed = jnp.zeros(leading + (block_count, block_width), jnp.float32)
    for offset in range(3):
        window = padded[..., offset:offset + block_count, :]
        summed = summed + jnp.einsum("kab,...kb->...ka", blocks[:, offset], window, precision=highest)
    return summed.reshape(values.shape)


def wall_derivative(values, matrix):
    return jnp.einsum("ab,fzbx->fzax", matrix, values, precision=highest)


def span_derivative(values, blocks):
    block_count = blocks.shape[0]
    block_width = blocks.shape[2]
    shaped = values.reshape((values.shape[0], block_count, block_width) + values.shape[2:])
    summed = jnp.zeros(shaped.shape, jnp.float32)
    for offset in range(3):
        rolled = jnp.roll(shaped, 1 - offset, axis=1)
        summed = summed + jnp.einsum("kab,fkbyx->fkayx", blocks[:, offset], rolled, precision=highest)
    return summed.reshape(values.shape)


def reference(conserved, register, stream_blocks, wall_matrix, span_blocks, inflow_gain, source_block, source_column):
    block_ids = jnp.arange(DEVICES, dtype=jnp.int32)[:, None]
    columns = jnp.arange(BLK_DEV, dtype=jnp.int32)[None, :]
    target_span = (block_ids % N_PZ) * CZ + columns // YROWS
    target_wall = (block_ids // N_PZ) * YROWS + columns % YROWS
    anchor = source_block[:, :, 0]
    anchor_span = (anchor % N_PZ) * CZ + source_column // YROWS
    anchor_wall = (anchor // N_PZ) * YROWS + source_column % YROWS
    recycle = conserved[:, :, :, XREC]
    fetched = recycle[:, anchor_span, anchor_wall] * inflow_gain[:, None, None]
    inlet_plane = jnp.zeros_like(recycle).at[:, target_span, target_wall].set(fetched)
    current = conserved.at[:, :, :, 0].set(inlet_plane)
    stream_term = stream_derivative(flux_set(current, 0), stream_blocks)
    wall_term = wall_derivative(flux_set(current, 1), wall_matrix)
    span_term = span_derivative(flux_set(current, 2), span_blocks)
    new_register = section_decay * register - time_step * (stream_term + wall_term + span_term)
    new_conserved = current + section_gain * new_register
    return new_conserved, new_register
```

```python
import functools

import jax
import jax.numpy as jnp
from jax import lax
from jax.experimental import pallas as pl
from jax.experimental.pallas import tpu as pltpu
from jax.sharding import PartitionSpec as P

highest = lax.Precision.HIGHEST
section_decay = -5.0 / 9.0
section_gain = 15.0 / 16.0
time_step = 0.1
vmem_limit = 48 * 1024 * 1024


def shift(values, axis, step):
    count = lax.axis_size(axis)
    return lax.ppermute(values, axis, [(i, (i + step) % count) for i in range(count)])


def flux_pieces(values, direction):
    inverse = 1.0 / values[0]
    speeds = [values[1 + d] * inverse for d in range(3)]
    pressure = 0.4 * (
        values[4] - 0.5 * (values[1] * speeds[0] + values[2] * speeds[1] + values[3] * speeds[2])
    )
    velocity = speeds[direction]
    pieces = [values[1 + direction]]
    for component in range(1, 4):
        moment = values[component] * velocity
        if component - 1 == direction:
            moment = moment + pressure
        pieces.append(moment)
    pieces.append((values[4] + pressure) * velocity)
    return pieces


def matmul(a, b):
    return jnp.dot(a, b, precision=highest, preferred_element_type=jnp.float32)


def wall_kernel(count, fields, place_ref, own_ref, *refs):
    received = refs[: count - 1]
    matrix_ref = refs[count - 1]
    outs = refs[count:]
    rows, cells = own_ref.shape[2:]
    sources = [own_ref] + list(received)
    lines = []
    for source in sources:
        lines.append(
            jnp.concatenate(flux_pieces([source[f, 0] for f in range(fields)], 1), axis=1)
        )
    term = matmul(matrix_ref[...], jnp.concatenate(lines, axis=0))
    for s, out in enumerate(outs):
        for f in range(fields):
            out[f, 0] = term[s * rows : (s + 1) * rows, f * cells : (f + 1) * cells]


def wall_part(place, conserved, received, matrix, offset, part):
    fields, span, rows, cells = conserved.shape
    count = len(received) + 1
    group = span // count
    block = (fields, 1, rows, cells)
    piece = pl.BlockSpec(block, lambda i, place: (0, i, 0, 0))
    return pl.pallas_call(
        functools.partial(wall_kernel, count, fields),
        out_shape=[jax.ShapeDtypeStruct((fields, part, rows, cells), jnp.float32)] * count,
        grid_spec=pltpu.PrefetchScalarGridSpec(
            num_scalar_prefetch=1,
            grid=(part,),
            in_specs=[pl.BlockSpec(block, lambda i, place: (0, place[0] * group + offset + i, 0, 0))]
            + [piece] * (count - 1)
            + [pl.BlockSpec(matrix.shape, lambda i, place: (0, 0))],
            out_specs=[piece] * count,
        ),
        compiler_params=pltpu.CompilerParams(vmem_limit_bytes=vmem_limit),
        cost_estimate=pl.CostEstimate(
            flops=12 * part * fields * cells * matrix.shape[0] ** 2,
            bytes_accessed=8 * count * fields * part * rows * cells,
            transcendentals=0,
        ),
        name="wall_part",
    )(place, conserved, *received, matrix)


def local_kernel(
    halo,
    cons_ref,
    before_ref,
    after_ref,
    reg_ref,
    inlet_ref,
    edge_ref,
    band_ref,
    stream_ref,
    current_ref,
    partial_ref,
    span_flux,
    stream_flux,
    span_out,
):
    fields, span, tile, cells = cons_ref.shape
    wide = span + 2 * halo
    lane = lax.broadcasted_iota(jnp.int32, (tile, cells), 1)
    for z in range(wide):
        if z < halo:
            source, at = before_ref, z
        elif z < halo + span:
            source, at = cons_ref, z - halo
        else:
            source, at = after_ref, z - halo - span
        values = [
            jnp.where(lane == 0, inlet_ref[f, :, z : z + 1], source[f, at]) for f in range(fields)
        ]
        for f, piece in enumerate(flux_pieces(values, 2)):
            for t in range(cells // 128):
                span_flux[t, pl.ds((f * wide + z) * tile, tile), :] = piece[:, t * 128 : t * 128 + 128]
        if source is cons_ref:
            for f, piece in enumerate(flux_pieces(values, 0)):
                stream_flux[pl.ds((f * span + at) * tile, tile), :] = piece
                current_ref[f, at] = values[f]
    band = band_ref[...]
    for f in range(fields):
        for y in range(tile):
            for t in range(cells // 128):
                lines = span_flux[t, pl.ds(f * wide * tile + y, wide, stride=tile), :]
                span_out[t, pl.ds(f * span * tile + y, span, stride=tile), :] = matmul(band, lines)
    weights = stream_ref[...]
    for f in range(fields):
        rows = pl.ds(f * span * tile, span * tile)
        beside = jnp.concatenate([span_out[t, rows, :] for t in range(cells // 128)], axis=1)
        total = matmul(stream_flux[rows, :], weights) + beside
        total = total.reshape(span, tile, cells)
        for z in range(span):
            term = total[z] + jnp.where(lane == 0, edge_ref[f, :, z : z + 1], 0.0)
            partial_ref[f, z] = section_decay * reg_ref[f, z] - time_step * term


def local_part(conserved, before, after, register, inlet, edge, band, weights):
    fields, span, rows, cells = conserved.shape
    halo = before.shape[1]
    wide = span + 2 * halo
    tile = 8
    main = pl.BlockSpec((fields, span, tile, cells), lambda i: (0, 0, i, 0))
    side = pl.BlockSpec((fields, halo, tile, cells), lambda i: (0, 0, i, 0))
    whole = lambda a: pl.BlockSpec(a.shape, lambda i: (0, 0))
    column = lambda a: pl.BlockSpec((fields, tile, a.shape[2]), lambda i: (0, i, 0))
    shape = jax.ShapeDtypeStruct(conserved.shape, jnp.float32)
    return pl.pallas_call(
        functools.partial(local_kernel, halo),
        out_shape=[shape, shape],
        grid=(rows // tile,),
        in_specs=[main, side, side, main, column(inlet), column(edge), whole(band), whole(weights)],
        out_specs=[main, main],
        scratch_shapes=[
            pltpu.VMEM((cells // 128, fields * wide * tile, 128), jnp.float32),
            pltpu.VMEM((fields * span * tile, cells), jnp.float32),
            pltpu.VMEM((cells // 128, fields * span * tile, 128), jnp.float32),
        ],
        compiler_params=pltpu.CompilerParams(vmem_limit_bytes=vmem_limit),
        cost_estimate=pl.CostEstimate(
            flops=12 * conserved.size * (cells + wide),
            bytes_accessed=20 * conserved.size,
            transcendentals=0,
        ),
        name="local_part",
    )(conserved, before, after, register, inlet, edge, band, weights)


def close_kernel(place_ref, current_ref, partial_ref, term_ref, cons_out, reg_out):
    lane = lax.broadcasted_iota(jnp.int32, term_ref.shape, 3)
    new = partial_ref[...] - time_step * jnp.where(lane == 0, 0.0, term_ref[...])
    reg_out[...] = new
    cons_out[...] = current_ref[...] + section_gain * new


def close_part(place, current, partial, term, group, offset):
    fields, part, rows, cells = term.shape
    block = (fields, 1, rows, cells)
    there = pl.BlockSpec(block, lambda i, place: (0, place[0] * group + offset + i, 0, 0))
    shape = jax.ShapeDtypeStruct(current.shape, jnp.float32)
    return pl.pallas_call(
        close_kernel,
        out_shape=[shape, shape],
        grid_spec=pltpu.PrefetchScalarGridSpec(
            num_scalar_prefetch=1,
            grid=(part,),
            in_specs=[there, there, pl.BlockSpec(block, lambda i, place: (0, i, 0, 0))],
            out_specs=[there, there],
        ),
        input_output_aliases={1: 0, 2: 1},
        compiler_params=pltpu.CompilerParams(vmem_limit_bytes=vmem_limit),
        cost_estimate=pl.CostEstimate(
            flops=4 * term.size, bytes_accessed=20 * term.size, transcendentals=0
        ),
        name="close_part",
    )(place, current, partial, term)


def stream_weights(blocks):
    count, _, width, _ = blocks.shape
    size = count * width
    full = jnp.zeros((size, size), jnp.float32)
    for k in range(count):
        for j in range(3):
            if 0 <= k + j - 1 < count:
                full = lax.dynamic_update_slice(full, blocks[k, j], (k * width, (k + j - 1) * width))
    return full.T


def span_band(blocks):
    count, _, width, _ = blocks.shape
    full = jnp.zeros((count * width, (count + 2) * width), jnp.float32)
    for k in range(count):
        for j in range(3):
            full = lax.dynamic_update_slice(full, blocks[k, j], (k * width, (k + j) * width))
    return full


def local(
    conserved,
    register,
    stream_blocks,
    wall_matrix,
    span_blocks,
    inflow_gain,
    source_block,
    source_column,
):
    fields, span, rows, cells = conserved.shape
    columns = span * rows
    count = lax.axis_size("py")
    across = lax.axis_size("pz")
    row = lax.axis_index("py")
    group = span // count
    parts = min(4, group)
    part = group // parts
    width = span_blocks.shape[2]
    place = lambda s: jnp.reshape((row + s) % count, (1,)).astype(jnp.int32)

    def outgoing(source, c):
        sent = []
        for s in range(1, count):
            start = ((row + s) % count) * group + c * part
            piece = lax.dynamic_slice_in_dim(source, start, part, 1)
            sent.append(shift(piece, "py", s))
        return sent

    received = [outgoing(conserved, 0)]

    recycle = conserved[:, :, :, 3 * cells // 4].reshape(-1, 128)
    recycle, later = lax.optimization_barrier((recycle, conserved))
    along = [recycle] + [shift(recycle, "py", s) for s in range(1, count)]
    for c in range(1, parts):
        received.append(outgoing(later, c))
    after = shift(later[:, :width], "pz", -1)
    before = shift(later[:, span - width :], "pz", 1)

    stacked = jnp.stack(along)
    whole_plane = lax.all_gather(stacked, "pz", axis=0)
    whole_plane = whole_plane.reshape(across, count, fields, columns)
    whole_plane = jnp.transpose(whole_plane, (2, 0, 1, 3)).reshape(fields, -1)
    myself = lax.axis_index(("py", "pz"))
    own_block = lax.dynamic_index_in_dim(source_block[:, :, 0], myself, 0, keepdims=False)
    own_column = lax.dynamic_index_in_dim(source_column, myself, 0, keepdims=False)
    slot = (own_block % across) * count + (row - own_block // across) % count
    fetched = jnp.take(whole_plane, slot * columns + own_column, axis=1)
    inlet = (fetched * inflow_gain[:, None]).reshape(fields, span, rows)

    inlet_after = shift(inlet[:, :width], "pz", -1)
    inlet_before = shift(inlet[:, span - width :], "pz", 1)
    lines = jnp.stack([inlet] + [shift(inlet, "py", s) for s in range(1, count)])
    order = (row - jnp.arange(count)) % count
    squares = wall_matrix.reshape(count, rows, count, rows)
    squares = jnp.take(jnp.take(squares, order, axis=0), order, axis=2)
    matrix = squares.reshape(wall_matrix.shape)
    line_flux = jnp.stack(flux_pieces([lines[:, f] for f in range(fields)], 1))
    edge = jnp.einsum("asb,fszb->faz", squares[0], line_flux, precision=highest)
    inlet_wide = jnp.concatenate([inlet_before, inlet, inlet_after], axis=1).swapaxes(1, 2)

    local_blocks = span // width
    own_blocks = lax.dynamic_slice_in_dim(
        span_blocks, lax.axis_index("pz") * local_blocks, local_blocks, 0
    )
    current, partial = local_part(
        conserved,
        before,
        after,
        register,
        inlet_wide,
        edge,
        span_band(own_blocks),
        stream_weights(stream_blocks),
    )

    returned = []
    for c in range(parts):
        pieces = wall_part(place(0), conserved, received[c], matrix, c * part, part)
        returned.append([pieces[0]] + [shift(pieces[s], "py", -s) for s in range(1, count)])
    for c in range(parts):
        for s in range(count):
            current, partial = close_part(
                place(s), current, partial, returned[c][s], group, c * part
            )
    return (current, partial)


def solution(mesh):
    return jax.shard_map(
        local,
        mesh=mesh,
        in_specs=(
            P(None, "pz", "py", None),
            P(None, "pz", "py", None),
            P(),
            P(),
            P(),
            P(),
            P(),
            P(),
        ),
        out_specs=(P(None, "pz", "py", None), P(None, "pz", "py", None)),
        check_vma=False,
    )
```

```python
import functools
import math

import jax
import jax.numpy as jnp
from jax import lax
from jax.experimental import pallas as pl
from jax.experimental.pallas import tpu as pltpu
from jax.sharding import PartitionSpec as P

highest = lax.Precision.HIGHEST
section_decay = -5.0 / 9.0
section_gain = 15.0 / 16.0
time_step = 0.1
vmem_limit = 48 * 1024 * 1024


def shift(values, axis, step):
    count = lax.axis_size(axis)
    return lax.ppermute(values, axis, [(i, (i + step) % count) for i in range(count)])


def after(values, *earlier):
    return lax.optimization_barrier((values, earlier))[0]


def order_of_steps(count):
    pairs = [(s, count - s) for s in range(1, (count + 1) // 2)]
    middle = [count // 2] if count % 2 == 0 and count > 1 else []
    return [s for pair in pairs for s in pair] + middle


def flux_pieces(values, direction):
    inverse = 1.0 / values[0]
    speeds = [values[1 + d] * inverse for d in range(3)]
    pressure = 0.4 * (
        values[4] - 0.5 * (values[1] * speeds[0] + values[2] * speeds[1] + values[3] * speeds[2])
    )
    velocity = speeds[direction]
    pieces = [values[1 + direction]]
    for component in range(1, 4):
        moment = values[component] * velocity
        if component - 1 == direction:
            moment = moment + pressure
        pieces.append(moment)
    pieces.append((values[4] + pressure) * velocity)
    return pieces


def matmul(a, b):
    return jnp.dot(a, b, precision=highest, preferred_element_type=jnp.float32)


def wall_kernel(count, fields, place_ref, own_ref, *refs):
    received = refs[: count - 1]
    matrix_ref = refs[count - 1]
    outs = refs[count:]
    rows, cells = own_ref.shape[2:]
    sources = [own_ref] + list(received)
    lines = []
    for source in sources:
        lines.append(
            jnp.concatenate(flux_pieces([source[f, 0] for f in range(fields)], 1), axis=1)
        )
    term = matmul(matrix_ref[...], jnp.concatenate(lines, axis=0))
    for s, out in enumerate(outs):
        for f in range(fields):
            out[f, 0] = term[s * rows : (s + 1) * rows, f * cells : (f + 1) * cells]


def wall_part(place, conserved, received, matrix, offset, part):
    fields, span, rows, cells = conserved.shape
    count = len(received) + 1
    group = span // count
    block = (fields, 1, rows, cells)
    piece = pl.BlockSpec(block, lambda i, place: (0, i, 0, 0))
    return pl.pallas_call(
        functools.partial(wall_kernel, count, fields),
        out_shape=[jax.ShapeDtypeStruct((fields, part, rows, cells), jnp.float32)] * count,
        grid_spec=pltpu.PrefetchScalarGridSpec(
            num_scalar_prefetch=1,
            grid=(part,),
            in_specs=[pl.BlockSpec(block, lambda i, place: (0, place[0] * group + offset + i, 0, 0))]
            + [piece] * (count - 1)
            + [pl.BlockSpec(matrix.shape, lambda i, place: (0, 0))],
            out_specs=[piece] * count,
        ),
        compiler_params=pltpu.CompilerParams(vmem_limit_bytes=vmem_limit),
        cost_estimate=pl.CostEstimate(
            flops=12 * part * fields * cells * matrix.shape[0] ** 2,
            bytes_accessed=8 * count * fields * part * rows * cells,
            transcendentals=0,
        ),
        name="wall_part",
    )(place, conserved, *received, matrix)


def inlet_kernel(table_ref, slot_ref, column_ref, gain_ref, out_ref, split):
    slots, fields, lines, lanes = table_ref.shape
    height = slots * lines

    @pl.when(pl.program_id(0) == 0)
    def _():
        for f in range(fields):
            rest = table_ref[:, f].reshape(height, lanes)
            for k in range(3):
                piece = rest.astype(jnp.bfloat16)
                split[k * fields + f] = piece.T
                rest = rest - piece.astype(jnp.float32)

    width = slot_ref.shape[1]
    column = column_ref[...]
    line = slot_ref[...] * lines + column // lanes
    choice = jnp.where(
        lax.broadcasted_iota(jnp.int32, (height, width), 0) == line, 1.0, 0.0
    ).astype(jnp.bfloat16)
    lane = lax.broadcasted_iota(jnp.int32, (lanes, width), 0) == column % lanes
    for f in range(fields):
        total = jnp.zeros((lanes, width), jnp.float32)
        for k in (2, 1, 0):
            total += jnp.dot(split[k * fields + f], choice, preferred_element_type=jnp.float32)
        picked = jnp.sum(jnp.where(lane, total, 0.0), axis=0, keepdims=True)
        out_ref[f : f + 1, :] = picked * gain_ref[f]


def inlet_part(table, slot, column, gain):
    slots, fields, lines, lanes = table.shape
    height = slots * lines
    columns = column.shape[1]
    width = math.gcd(columns, 512)
    row = pl.BlockSpec((1, width), lambda i: (0, i))
    return pl.pallas_call(
        inlet_kernel,
        out_shape=jax.ShapeDtypeStruct((fields, columns), jnp.float32),
        grid=(columns // width,),
        in_specs=[
            pl.BlockSpec(table.shape, lambda i: (0, 0, 0, 0)),
            row,
            row,
            pl.BlockSpec(memory_space=pltpu.SMEM),
        ],
        out_specs=pl.BlockSpec((fields, width), lambda i: (0, i)),
        scratch_shapes=[pltpu.VMEM((3 * fields, lanes, height), jnp.bfloat16)],
        compiler_params=pltpu.CompilerParams(vmem_limit_bytes=vmem_limit),
        cost_estimate=pl.CostEstimate(
            flops=6 * fields * lanes * height * columns,
            bytes_accessed=4 * table.size,
            transcendentals=0,
        ),
        name="inlet_part",
    )(table, slot, column, gain)


def local_kernel(
    halo,
    cons_ref,
    before_ref,
    after_ref,
    reg_ref,
    inlet_ref,
    edge_ref,
    band_ref,
    stream_ref,
    current_ref,
    partial_ref,
    span_flux,
    stream_flux,
    span_out,
):
    fields, span, tile, cells = cons_ref.shape
    wide = span + 2 * halo
    lane = lax.broadcasted_iota(jnp.int32, (tile, cells), 1)
    for z in range(wide):
        if z < halo:
            source, at = before_ref, z
        elif z < halo + span:
            source, at = cons_ref, z - halo
        else:
            source, at = after_ref, z - halo - span
        values = [
            jnp.where(lane == 0, inlet_ref[f, :, z : z + 1], source[f, at]) for f in range(fields)
        ]
        for f, piece in enumerate(flux_pieces(values, 2)):
            for t in range(cells // 128):
                span_flux[t, pl.ds((f * wide + z) * tile, tile), :] = piece[:, t * 128 : t * 128 + 128]
        if source is cons_ref:
            for f, piece in enumerate(flux_pieces(values, 0)):
                stream_flux[pl.ds((f * span + at) * tile, tile), :] = piece
                current_ref[f, at] = values[f]
    band = band_ref[...]
    for f in range(fields):
        for y in range(tile):
            for t in range(cells // 128):
                lines = span_flux[t, pl.ds(f * wide * tile + y, wide, stride=tile), :]
                span_out[t, pl.ds(f * span * tile + y, span, stride=tile), :] = matmul(band, lines)
    weights = stream_ref[...]
    for f in range(fields):
        rows = pl.ds(f * span * tile, span * tile)
        beside = jnp.concatenate([span_out[t, rows, :] for t in range(cells // 128)], axis=1)
        total = matmul(stream_flux[rows, :], weights) + beside
        total = total.reshape(span, tile, cells)
        for z in range(span):
            term = total[z] + jnp.where(lane == 0, edge_ref[f, :, z : z + 1], 0.0)
            partial_ref[f, z] = section_decay * reg_ref[f, z] - time_step * term


def local_part(conserved, before, after, register, inlet, edge, band, weights):
    fields, span, rows, cells = conserved.shape
    halo = before.shape[1]
    wide = span + 2 * halo
    tile = 8
    main = pl.BlockSpec((fields, span, tile, cells), lambda i: (0, 0, i, 0))
    side = pl.BlockSpec((fields, halo, tile, cells), lambda i: (0, 0, i, 0))
    whole = lambda a: pl.BlockSpec(a.shape, lambda i: (0, 0))
    column = lambda a: pl.BlockSpec((fields, tile, a.shape[2]), lambda i: (0, i, 0))
    shape = jax.ShapeDtypeStruct(conserved.shape, jnp.float32)
    return pl.pallas_call(
        functools.partial(local_kernel, halo),
        out_shape=[shape, shape],
        grid=(rows // tile,),
        in_specs=[main, side, side, main, column(inlet), column(edge), whole(band), whole(weights)],
        out_specs=[main, main],
        scratch_shapes=[
            pltpu.VMEM((cells // 128, fields * wide * tile, 128), jnp.float32),
            pltpu.VMEM((fields * span * tile, cells), jnp.float32),
            pltpu.VMEM((cells // 128, fields * span * tile, 128), jnp.float32),
        ],
        compiler_params=pltpu.CompilerParams(vmem_limit_bytes=vmem_limit),
        cost_estimate=pl.CostEstimate(
            flops=12 * conserved.size * (cells + wide),
            bytes_accessed=20 * conserved.size,
            transcendentals=0,
        ),
        name="local_part",
    )(conserved, before, after, register, inlet, edge, band, weights)


def close_kernel(place_ref, current_ref, partial_ref, term_ref, cons_out, reg_out):
    lane = lax.broadcasted_iota(jnp.int32, term_ref.shape, 3)
    new = partial_ref[...] - time_step * jnp.where(lane == 0, 0.0, term_ref[...])
    reg_out[...] = new
    cons_out[...] = current_ref[...] + section_gain * new


def close_part(place, current, partial, term, group, offset):
    fields, part, rows, cells = term.shape
    step = math.gcd(part, 4)
    block = (fields, step, rows, cells)
    there = pl.BlockSpec(
        block, lambda i, place: (0, (place[0] * group + offset) // step + i, 0, 0)
    )
    shape = jax.ShapeDtypeStruct(current.shape, jnp.float32)
    return pl.pallas_call(
        close_kernel,
        out_shape=[shape, shape],
        grid_spec=pltpu.PrefetchScalarGridSpec(
            num_scalar_prefetch=1,
            grid=(part // step,),
            in_specs=[there, there, pl.BlockSpec(block, lambda i, place: (0, i, 0, 0))],
            out_specs=[there, there],
        ),
        input_output_aliases={1: 0, 2: 1},
        compiler_params=pltpu.CompilerParams(vmem_limit_bytes=vmem_limit),
        cost_estimate=pl.CostEstimate(
            flops=4 * term.size, bytes_accessed=20 * term.size, transcendentals=0
        ),
        name="close_part",
    )(place, current, partial, term)


def stream_weights(blocks):
    count, _, width, _ = blocks.shape
    size = count * width
    full = jnp.zeros((size, size), jnp.float32)
    for k in range(count):
        for j in range(3):
            if 0 <= k + j - 1 < count:
                full = lax.dynamic_update_slice(full, blocks[k, j], (k * width, (k + j - 1) * width))
    return full.T


def span_band(blocks):
    count, _, width, _ = blocks.shape
    full = jnp.zeros((count * width, (count + 2) * width), jnp.float32)
    for k in range(count):
        for j in range(3):
            full = lax.dynamic_update_slice(full, blocks[k, j], (k * width, (k + j) * width))
    return full


def local(
    conserved,
    register,
    stream_blocks,
    wall_matrix,
    span_blocks,
    inflow_gain,
    source_block,
    source_column,
):
    fields, span, rows, cells = conserved.shape
    columns = span * rows
    count = lax.axis_size("py")
    across = lax.axis_size("pz")
    row = lax.axis_index("py")
    group = span // count
    parts = min(2, group)
    part = group // parts
    width = span_blocks.shape[2]
    steps = order_of_steps(count)
    place = lambda s: jnp.reshape((row + s) % count, (1,)).astype(jnp.int32)

    def outgoing(source, c, s):
        start = ((row - s) % count) * group + c * part
        return lax.dynamic_slice_in_dim(source, start, part, 1)

    first = {s: outgoing(conserved, 0, s) for s in steps}
    early, late = steps[:2], steps[2:]
    received = [{s: shift(first[s], "py", -s) for s in early}, {}]

    behind = after(conserved, *[first[s] for s in early])
    recycle = behind[:, :, :, 3 * cells // 4].reshape(-1, 128)
    along = [recycle] + [shift(recycle, "py", -s) for s in range(1, count)]
    rest = after(conserved, recycle)
    second = {s: outgoing(rest, parts - 1, s) for s in steps}
    head, tail = after((rest[:, :width], rest[:, span - width :]), *along)
    for s in late:
        received[0][s] = shift(after(first[s], received[0][early[0]]), "py", -s)
    waits = [received[0][s] for s in steps[1:]]
    for s, wait in zip(steps, waits + [waits[-1]] * count):
        received[1][s] = shift(after(second[s], wait), "py", -s)
    halo_after = shift(head, "pz", -1)
    halo_before = shift(tail, "pz", 1)

    table = lax.all_gather(jnp.stack(along), "pz", axis=0).reshape(across * count, fields, -1, 128)
    myself = lax.axis_index(("py", "pz"))
    own_block = lax.dynamic_slice_in_dim(source_block[:, :, 0], myself, 1, 0)
    own_column = lax.dynamic_slice_in_dim(source_column, myself, 1, 0)
    slot = (own_block % across) * count + (own_block // across - row) % count

    twice = jnp.concatenate([wall_matrix, wall_matrix], axis=0)
    twice = lax.dynamic_slice_in_dim(twice, row * rows, count * rows, 0)
    twice = jnp.concatenate([twice, twice], axis=1)
    matrix = lax.dynamic_slice_in_dim(twice, row * rows, count * rows, 1)

    returned = [{}, {}]
    pieces = wall_part(
        place(0), conserved, [received[0][s] for s in range(1, count)], matrix, 0, part
    )
    returned[0][0] = pieces[0]
    waits = [received[1][s] for s in steps]
    for s, wait in zip(steps, waits[:-1] + [waits[-2]] * count):
        returned[0][s] = shift(after(pieces[s], wait), "py", s)

    inlet = inlet_part(table, slot, own_column, inflow_gain).reshape(fields, span, rows)

    inlet_after = shift(inlet[:, :width], "pz", -1)
    inlet_before = shift(inlet[:, span - width :], "pz", 1)
    flat = inlet.reshape(-1, 128)
    lines = lax.all_to_all(
        jnp.broadcast_to(flat, (count,) + flat.shape), "py", split_axis=0, concat_axis=0
    )
    lines = lines.reshape(count, fields, span, rows)
    line_flux = jnp.stack(flux_pieces([lines[:, f] for f in range(fields)], 1))
    own_rows = lax.dynamic_slice_in_dim(wall_matrix, row * rows, rows, 0)
    edge = jnp.einsum(
        "asb,fszb->faz", own_rows.reshape(rows, count, rows), line_flux, precision=highest
    )
    inlet_wide = jnp.concatenate([inlet_before, inlet, inlet_after], axis=1).swapaxes(1, 2)

    local_blocks = span // width
    own_blocks = lax.dynamic_slice_in_dim(
        span_blocks, lax.axis_index("pz") * local_blocks, local_blocks, 0
    )

    pieces = wall_part(
        place(0),
        conserved,
        [received[1][s] for s in range(1, count)],
        matrix,
        (parts - 1) * part,
        part,
    )
    returned[1][0] = pieces[0]
    waits = [returned[0][s] for s in steps]
    for s, wait in zip(steps, waits[:-1] + [waits[-2]] * count):
        returned[1][s] = shift(after(pieces[s], wait), "py", s)

    current, partial = local_part(
        conserved,
        halo_before,
        halo_after,
        register,
        inlet_wide,
        edge,
        span_band(own_blocks),
        stream_weights(stream_blocks),
    )
    for c in range(parts):
        for s in [0] + steps:
            current, partial = close_part(
                place(-s), current, partial, returned[c][s], group, c * part
            )
    return (current, partial)


def solution(mesh):
    return jax.shard_map(
        local,
        mesh=mesh,
        in_specs=(
            P(None, "pz", "py", None),
            P(None, "pz", "py", None),
            P(),
            P(),
            P(),
            P(),
            P(),
            P(),
        ),
        out_specs=(P(None, "pz", "py", None), P(None, "pz", "py", None)),
        check_vma=False,
    )
```

```python
import functools
import math

import jax
import jax.numpy as jnp
from jax import lax
from jax.experimental import pallas as pl
from jax.experimental.pallas import tpu as pltpu
from jax.sharding import PartitionSpec as P

highest = lax.Precision.HIGHEST
section_decay = -5.0 / 9.0
section_gain = 15.0 / 16.0
time_step = 0.1
vmem_limit = 48 * 1024 * 1024
small_cost = pl.CostEstimate(flops=1, bytes_accessed=1, transcendentals=0)


def shift(values, axis, step):
    count = lax.axis_size(axis)
    return lax.ppermute(values, axis, [(i, (i + step) % count) for i in range(count)])


def after(values, *earlier):
    return lax.optimization_barrier((values, earlier))[0]


def order_of_steps(count):
    pairs = [(s, count - s) for s in range(1, (count + 1) // 2)]
    middle = [count // 2] if count % 2 == 0 and count > 1 else []
    return [s for pair in pairs for s in pair] + middle


def flux_pieces(values, direction):
    inverse = 1.0 / values[0]
    speeds = [values[1 + d] * inverse for d in range(3)]
    pressure = 0.4 * (
        values[4] - 0.5 * (values[1] * speeds[0] + values[2] * speeds[1] + values[3] * speeds[2])
    )
    velocity = speeds[direction]
    pieces = [values[1 + direction]]
    for component in range(1, 4):
        moment = values[component] * velocity
        if component - 1 == direction:
            moment = moment + pressure
        pieces.append(moment)
    pieces.append((values[4] + pressure) * velocity)
    return pieces


def matmul(a, b):
    return jnp.dot(a, b, precision=highest, preferred_element_type=jnp.float32)


def wall_kernel(count, fields, place_ref, own_ref, *refs):
    received = refs[: count - 1]
    matrix_ref = refs[count - 1]
    outs = refs[count:]
    rows, cells = own_ref.shape[2:]
    sources = [own_ref] + list(received)
    lines = []
    for source in sources:
        lines.append(
            jnp.concatenate(flux_pieces([source[f, 0] for f in range(fields)], 1), axis=1)
        )
    term = matmul(matrix_ref[...], jnp.concatenate(lines, axis=0))
    for s, out in enumerate(outs):
        for f in range(fields):
            out[f, 0] = term[s * rows : (s + 1) * rows, f * cells : (f + 1) * cells]


def wall_part(place, conserved, received, matrix, offset, part):
    fields, span, rows, cells = conserved.shape
    count = len(received) + 1
    group = span // count
    block = (fields, 1, rows, cells)
    piece = pl.BlockSpec(block, lambda i, place: (0, i, 0, 0))
    within = pl.BlockSpec(block, lambda i, place: (0, offset + i, 0, 0))
    return pl.pallas_call(
        functools.partial(wall_kernel, count, fields),
        out_shape=[jax.ShapeDtypeStruct((fields, part, rows, cells), jnp.float32)] * count,
        grid_spec=pltpu.PrefetchScalarGridSpec(
            num_scalar_prefetch=1,
            grid=(part,),
            in_specs=[pl.BlockSpec(block, lambda i, place: (0, place[0] * group + offset + i, 0, 0))]
            + [piece if a.shape[1] == part else within for a in received]
            + [pl.BlockSpec(matrix.shape, lambda i, place: (0, 0))],
            out_specs=[piece] * count,
        ),
        compiler_params=pltpu.CompilerParams(vmem_limit_bytes=vmem_limit),
        cost_estimate=small_cost,
        name="wall_part",
    )(place, conserved, *received, matrix)


def inlet_kernel(table_ref, slot_ref, column_ref, gain_ref, out_ref, split):
    slots, fields, lines, lanes = table_ref.shape
    height = slots * lines

    @pl.when(pl.program_id(0) == 0)
    def _():
        for f in range(fields):
            rest = table_ref[:, f].reshape(height, lanes)
            for k in range(3):
                piece = rest.astype(jnp.bfloat16)
                split[k * fields + f] = piece.T
                rest = rest - piece.astype(jnp.float32)

    width = slot_ref.shape[1]
    column = column_ref[...]
    line = slot_ref[...] * lines + column // lanes
    choice = jnp.where(
        lax.broadcasted_iota(jnp.int32, (height, width), 0) == line, 1.0, 0.0
    ).astype(jnp.bfloat16)
    lane = lax.broadcasted_iota(jnp.int32, (lanes, width), 0) == column % lanes
    for f in range(fields):
        total = jnp.zeros((lanes, width), jnp.float32)
        for k in (2, 1, 0):
            total += jnp.dot(split[k * fields + f], choice, preferred_element_type=jnp.float32)
        picked = jnp.sum(jnp.where(lane, total, 0.0), axis=0, keepdims=True)
        out_ref[f : f + 1, :] = picked * gain_ref[f]


def inlet_part(table, slot, column, gain):
    slots, fields, lines, lanes = table.shape
    height = slots * lines
    columns = column.shape[1]
    width = math.gcd(columns, 512)
    row = pl.BlockSpec((1, width), lambda i: (0, i))
    return pl.pallas_call(
        inlet_kernel,
        out_shape=jax.ShapeDtypeStruct((fields, columns), jnp.float32),
        grid=(columns // width,),
        in_specs=[
            pl.BlockSpec(table.shape, lambda i: (0, 0, 0, 0)),
            row,
            row,
            pl.BlockSpec(memory_space=pltpu.SMEM),
        ],
        out_specs=pl.BlockSpec((fields, width), lambda i: (0, i)),
        scratch_shapes=[pltpu.VMEM((3 * fields, lanes, height), jnp.bfloat16)],
        compiler_params=pltpu.CompilerParams(vmem_limit_bytes=vmem_limit),
        cost_estimate=small_cost,
        name="inlet_part",
    )(table, slot, column, gain)


def local_kernel(
    halo,
    cons_ref,
    before_ref,
    after_ref,
    reg_ref,
    inlet_ref,
    edge_ref,
    band_ref,
    stream_ref,
    current_ref,
    partial_ref,
    span_flux,
    stream_flux,
    span_out,
):
    fields, span, tile, cells = cons_ref.shape
    wide = span + 2 * halo
    lane = lax.broadcasted_iota(jnp.int32, (tile, cells), 1)
    for z in range(wide):
        if z < halo:
            source, at = before_ref, z
        elif z < halo + span:
            source, at = cons_ref, z - halo
        else:
            source, at = after_ref, z - halo - span
        values = [
            jnp.where(lane == 0, inlet_ref[f, :, z : z + 1], source[f, at]) for f in range(fields)
        ]
        for f, piece in enumerate(flux_pieces(values, 2)):
            for t in range(cells // 128):
                span_flux[t, pl.ds((f * wide + z) * tile, tile), :] = piece[:, t * 128 : t * 128 + 128]
        if source is cons_ref:
            for f, piece in enumerate(flux_pieces(values, 0)):
                stream_flux[pl.ds((f * span + at) * tile, tile), :] = piece
                current_ref[f, at] = values[f]
    band = band_ref[...]
    for f in range(fields):
        for y in range(tile):
            for t in range(cells // 128):
                lines = span_flux[t, pl.ds(f * wide * tile + y, wide, stride=tile), :]
                span_out[t, pl.ds(f * span * tile + y, span, stride=tile), :] = matmul(band, lines)
    weights = stream_ref[...]
    for f in range(fields):
        rows = pl.ds(f * span * tile, span * tile)
        beside = jnp.concatenate([span_out[t, rows, :] for t in range(cells // 128)], axis=1)
        total = matmul(stream_flux[rows, :], weights) + beside
        total = total.reshape(span, tile, cells)
        for z in range(span):
            term = total[z] + jnp.where(lane == 0, edge_ref[f, :, z : z + 1], 0.0)
            partial_ref[f, z] = section_decay * reg_ref[f, z] - time_step * term


def local_part(conserved, before, after, register, inlet, edge, band, weights):
    fields, span, rows, cells = conserved.shape
    halo = before.shape[1]
    wide = span + 2 * halo
    tile = 8
    main = pl.BlockSpec((fields, span, tile, cells), lambda i: (0, 0, i, 0))
    side = pl.BlockSpec((fields, halo, tile, cells), lambda i: (0, 0, i, 0))
    whole = lambda a: pl.BlockSpec(a.shape, lambda i: (0, 0))
    column = lambda a: pl.BlockSpec((fields, tile, a.shape[2]), lambda i: (0, i, 0))
    shape = jax.ShapeDtypeStruct(conserved.shape, jnp.float32)
    return pl.pallas_call(
        functools.partial(local_kernel, halo),
        out_shape=[shape, shape],
        grid=(rows // tile,),
        in_specs=[main, side, side, main, column(inlet), column(edge), whole(band), whole(weights)],
        out_specs=[main, main],
        scratch_shapes=[
            pltpu.VMEM((cells // 128, fields * wide * tile, 128), jnp.float32),
            pltpu.VMEM((fields * span * tile, cells), jnp.float32),
            pltpu.VMEM((cells // 128, fields * span * tile, 128), jnp.float32),
        ],
        compiler_params=pltpu.CompilerParams(vmem_limit_bytes=vmem_limit),
        cost_estimate=small_cost,
        name="local_part",
    )(conserved, before, after, register, inlet, edge, band, weights)


def close_kernel(place_ref, current_ref, partial_ref, term_ref, cons_out, reg_out):
    lane = lax.broadcasted_iota(jnp.int32, term_ref.shape, 3)
    new = partial_ref[...] - time_step * jnp.where(lane == 0, 0.0, term_ref[...])
    reg_out[...] = new
    cons_out[...] = current_ref[...] + section_gain * new


def close_part(place, current, partial, term, group, offset):
    fields, part, rows, cells = term.shape
    step = math.gcd(part, 4)
    block = (fields, step, rows, cells)
    there = pl.BlockSpec(
        block, lambda i, place: (0, (place[0] * group + offset) // step + i, 0, 0)
    )
    shape = jax.ShapeDtypeStruct(current.shape, jnp.float32)
    return pl.pallas_call(
        close_kernel,
        out_shape=[shape, shape],
        grid_spec=pltpu.PrefetchScalarGridSpec(
            num_scalar_prefetch=1,
            grid=(part // step,),
            in_specs=[there, there, pl.BlockSpec(block, lambda i, place: (0, i, 0, 0))],
            out_specs=[there, there],
        ),
        input_output_aliases={1: 0, 2: 1},
        compiler_params=pltpu.CompilerParams(vmem_limit_bytes=vmem_limit),
        cost_estimate=small_cost,
        name="close_part",
    )(place, current, partial, term)


def stream_weights(blocks):
    count, _, width, _ = blocks.shape
    size = count * width
    full = jnp.zeros((size, size), jnp.float32)
    for k in range(count):
        for j in range(3):
            if 0 <= k + j - 1 < count:
                full = lax.dynamic_update_slice(full, blocks[k, j], (k * width, (k + j - 1) * width))
    return full.T


def span_band(blocks):
    count, _, width, _ = blocks.shape
    full = jnp.zeros((count * width, (count + 2) * width), jnp.float32)
    for k in range(count):
        for j in range(3):
            full = lax.dynamic_update_slice(full, blocks[k, j], (k * width, (k + j) * width))
    return full


def local(
    conserved,
    register,
    stream_blocks,
    wall_matrix,
    span_blocks,
    inflow_gain,
    source_block,
    source_column,
):
    fields, span, rows, cells = conserved.shape
    columns = span * rows
    count = lax.axis_size("py")
    across = lax.axis_size("pz")
    row = lax.axis_index("py")
    group = span // count
    parts = min(2, group)
    part = group // parts
    width = span_blocks.shape[2]
    steps = order_of_steps(count)
    place = lambda s: jnp.reshape((row + s) % count, (1,)).astype(jnp.int32)

    def outgoing(source, s, offset, length):
        start = ((row - s) % count) * group + offset
        return lax.dynamic_slice_in_dim(source, start, length, 1)

    piece = outgoing(conserved, steps[0], 0, group)
    received = {steps[0]: shift(piece, "py", -steps[0])}
    behind = after(conserved, piece)
    for s in steps[1:-1]:
        received[s] = shift(outgoing(behind, s, 0, group), "py", -s)
    pieces = [outgoing(behind, steps[-1], c * part, part) for c in range(parts)]
    ahead = [received[steps[0]]]
    last = [shift(pieces[0], "py", -steps[-1])]
    for c in range(1, parts):
        last.append(shift(after(pieces[c], ahead[-1]), "py", -steps[-1]))
    head, tail = after((conserved[:, :width], conserved[:, span - width :]), *pieces)
    halo_after = shift(head, "pz", -1)
    halo_before = shift(tail, "pz", 1)

    recycle = after(conserved, received[steps[0]])
    recycle = recycle[:, :, :, 3 * cells // 4].reshape(-1, 128)
    along = lax.all_to_all(
        jnp.broadcast_to(recycle, (count,) + recycle.shape), "py", split_axis=0, concat_axis=0
    )
    table = lax.all_gather(along, "pz", axis=0).reshape(across * count, fields, -1, 128)

    place_of = lambda a: lax.dynamic_index_in_dim(
        a.reshape(count, across, columns), lax.axis_index("pz"), 1, keepdims=False
    )
    beside = lambda a, step: lax.dynamic_index_in_dim(
        lax.dynamic_index_in_dim(a.reshape(count, across, columns), row, 0, keepdims=False),
        (lax.axis_index("pz") + step) % across,
        0,
        keepdims=False,
    )
    edge_columns = width * rows

    def sources(a):
        lines = place_of(a)
        lines = lax.dynamic_slice_in_dim(jnp.concatenate([lines, lines]), row, count, 0)
        near = jnp.concatenate(
            [beside(a, -1)[columns - edge_columns :], lines[0], beside(a, 1)[:edge_columns]]
        )
        return near.reshape(1, -1), lines[1:].reshape(1, -1)

    near_block, far_block = sources(source_block)
    near_column, far_column = sources(source_column)
    slot = lambda block: (block % across) * count + block // across

    twice = jnp.concatenate([wall_matrix, wall_matrix], axis=0)
    twice = lax.dynamic_slice_in_dim(twice, row * rows, count * rows, 0)
    twice = jnp.concatenate([twice, twice], axis=1)
    matrix = lax.dynamic_slice_in_dim(twice, row * rows, count * rows, 1)

    def wall(c, *earlier):
        parted = {**received, steps[-1]: last[c]}
        return wall_part(
            place(0),
            conserved,
            [parted[s] for s in range(1, count)],
            after(matrix, *earlier),
            c * part,
            part,
        )

    pieces = wall(0)
    returned = [{0: pieces[0]}, {}]
    waits = [halo_after, halo_before] + [halo_after] * count
    for s, wait in zip(steps, waits):
        returned[0][s] = shift(after(pieces[s], wait), "py", s)

    near = inlet_part(table, slot(near_block), after(near_column, pieces[0]), inflow_gain)
    inlet_wide = near.reshape(fields, span + 2 * width, rows).swapaxes(1, 2)
    far = inlet_part(table, slot(far_block), after(far_column, near), inflow_gain)

    pieces = wall(parts - 1, far)
    returned[1][0] = pieces[0]
    for k, s in enumerate(steps):
        piece = pieces[s]
        if k >= 2:
            piece = after(piece, returned[0][steps[k - 2]])
        returned[1][s] = shift(piece, "py", s)

    own = near.reshape(fields, span + 2 * width, rows)[:, width : width + span]
    lines = jnp.concatenate(
        [own[:, None], far.reshape(fields, count - 1, span, rows)], axis=1
    )
    line_flux = jnp.stack(flux_pieces([lines[f] for f in range(fields)], 1))
    edge = jnp.einsum(
        "asb,fszb->faz", matrix[:rows].reshape(rows, count, rows), line_flux, precision=highest
    )

    local_blocks = span // width
    own_blocks = lax.dynamic_slice_in_dim(
        span_blocks, lax.axis_index("pz") * local_blocks, local_blocks, 0
    )

    current, partial = local_part(
        conserved,
        halo_before,
        halo_after,
        register,
        inlet_wide,
        edge,
        span_band(own_blocks),
        stream_weights(stream_blocks),
    )
    for c in range(parts):
        for s in [0] + steps:
            current, partial = close_part(
                place(-s), current, partial, returned[c][s], group, c * part
            )
    return (current, partial)


def solution(mesh):
    return jax.shard_map(
        local,
        mesh=mesh,
        in_specs=(
            P(None, "pz", "py", None),
            P(None, "pz", "py", None),
            P(),
            P(),
            P(),
            P(),
            P(),
            P(),
        ),
        out_specs=(P(None, "pz", "py", None), P(None, "pz", "py", None)),
        check_vma=False,
    )
```

```python
import functools
import math

import jax
import jax.numpy as jnp
from jax import lax
from jax.experimental import pallas as pl
from jax.experimental.pallas import tpu as pltpu
from jax.sharding import PartitionSpec as P

highest = lax.Precision.HIGHEST
section_decay = -5.0 / 9.0
section_gain = 15.0 / 16.0
time_step = 0.1
vmem_limit = 48 * 1024 * 1024
small_cost = pl.CostEstimate(flops=1, bytes_accessed=1, transcendentals=0)


def shift(values, axis, step):
    count = lax.axis_size(axis)
    return lax.ppermute(values, axis, [(i, (i + step) % count) for i in range(count)])


def after(values, *earlier):
    return lax.optimization_barrier((values, earlier))[0]


def order_of_steps(count):
    pairs = [(s, count - s) for s in range(1, (count + 1) // 2)]
    middle = [count // 2] if count % 2 == 0 and count > 1 else []
    return [s for pair in pairs for s in pair] + middle


def flux_pieces(values, direction):
    inverse = 1.0 / values[0]
    speeds = [values[1 + d] * inverse for d in range(3)]
    pressure = 0.4 * (
        values[4] - 0.5 * (values[1] * speeds[0] + values[2] * speeds[1] + values[3] * speeds[2])
    )
    velocity = speeds[direction]
    pieces = [values[1 + direction]]
    for component in range(1, 4):
        moment = values[component] * velocity
        if component - 1 == direction:
            moment = moment + pressure
        pieces.append(moment)
    pieces.append((values[4] + pressure) * velocity)
    return pieces


def matmul(a, b):
    return jnp.dot(a, b, precision=highest, preferred_element_type=jnp.float32)


def wall_kernel(count, fields, place_ref, own_ref, *refs):
    received = refs[: count - 1]
    matrix_ref = refs[count - 1]
    outs = refs[count:]
    rows, cells = own_ref.shape[2:]
    sources = [own_ref] + list(received)
    lines = []
    for source in sources:
        lines.append(
            jnp.concatenate(flux_pieces([source[f, 0] for f in range(fields)], 1), axis=1)
        )
    term = matmul(matrix_ref[...], jnp.concatenate(lines, axis=0))
    for s, out in enumerate(outs):
        for f in range(fields):
            out[f, 0] = term[s * rows : (s + 1) * rows, f * cells : (f + 1) * cells]


def wall_part(place, conserved, received, matrix, offset, part):
    fields, span, rows, cells = conserved.shape
    count = len(received) + 1
    group = span // count
    block = (fields, 1, rows, cells)
    piece = pl.BlockSpec(block, lambda i, place: (0, i, 0, 0))
    within = lambda a: piece if a.shape[1] == part else whole
    whole = pl.BlockSpec(block, lambda i, place: (0, offset + i, 0, 0))
    return pl.pallas_call(
        functools.partial(wall_kernel, count, fields),
        out_shape=[jax.ShapeDtypeStruct((fields, part, rows, cells), jnp.float32)] * count,
        grid_spec=pltpu.PrefetchScalarGridSpec(
            num_scalar_prefetch=1,
            grid=(part,),
            in_specs=[pl.BlockSpec(block, lambda i, place: (0, place[0] * group + offset + i, 0, 0))]
            + [within(a) for a in received]
            + [pl.BlockSpec(matrix.shape, lambda i, place: (0, 0))],
            out_specs=[piece] * count,
        ),
        compiler_params=pltpu.CompilerParams(vmem_limit_bytes=vmem_limit),
        cost_estimate=small_cost,
        name="wall_part",
    )(place, conserved, *received, matrix)


def inlet_kernel(table_ref, source_ref, gain_ref, out_ref, split):
    slots, fields, lines, lanes = table_ref.shape
    height = slots * lines

    @pl.when(pl.program_id(0) == 0)
    def _():
        for f in range(fields):
            rest = table_ref[:, f].reshape(height, lanes)
            for k in range(3):
                piece = rest.astype(jnp.bfloat16)
                split[pl.ds((k * fields + f) * lanes, lanes), :] = piece.T
                rest = rest - piece.astype(jnp.float32)

    width = source_ref.shape[1]
    source = source_ref[...]
    line = source // lanes
    choice = jnp.where(
        lax.broadcasted_iota(jnp.int32, (height, width), 0) == line, 1.0, 0.0
    ).astype(jnp.bfloat16)
    lane = lax.broadcasted_iota(jnp.int32, (lanes, width), 0) == source % lanes
    found = jnp.dot(split[...], choice, preferred_element_type=jnp.float32)
    found = found.reshape(3, fields, lanes, width)
    for f in range(fields):
        total = found[2, f] + found[1, f] + found[0, f]
        picked = jnp.sum(jnp.where(lane, total, 0.0), axis=0, keepdims=True)
        picked = picked * gain_ref[f]
        for k in range(width // lanes):
            out_ref[f, k : k + 1, :] = picked[:, k * lanes : (k + 1) * lanes]


def inlet_part(table, source, gain):
    slots, fields, lines, lanes = table.shape
    height = slots * lines
    columns = source.shape[1]
    width = 8 * lanes
    row = pl.BlockSpec((1, width), lambda i: (0, i))
    return pl.pallas_call(
        inlet_kernel,
        out_shape=jax.ShapeDtypeStruct((fields, columns // lanes, lanes), jnp.float32),
        grid=(columns // width,),
        in_specs=[
            pl.BlockSpec(table.shape, lambda i: (0, 0, 0, 0)),
            row,
            pl.BlockSpec(memory_space=pltpu.SMEM),
        ],
        out_specs=pl.BlockSpec((fields, 8, lanes), lambda i: (0, i, 0)),
        scratch_shapes=[pltpu.VMEM((3 * fields * lanes, height), jnp.bfloat16)],
        compiler_params=pltpu.CompilerParams(vmem_limit_bytes=vmem_limit),
        cost_estimate=small_cost,
        name="inlet_part",
    )(table, source, gain)


def local_kernel(
    halo,
    cons_ref,
    before_ref,
    after_ref,
    reg_ref,
    inlet_ref,
    near_ref,
    far_ref,
    matrix_ref,
    band_ref,
    stream_ref,
    current_ref,
    partial_ref,
    span_flux,
    stream_flux,
    span_out,
):
    fields, span, tile, cells = cons_ref.shape
    wide = span + 2 * halo
    lane = lax.broadcasted_iota(jnp.int32, (tile, cells), 1)
    for z in range(wide):
        if z < halo:
            source, at = before_ref, z
        elif z < halo + span:
            source, at = cons_ref, z - halo
        else:
            source, at = after_ref, z - halo - span
        values = [
            jnp.where(lane == 0, inlet_ref[f, :, z : z + 1], source[f, at]) for f in range(fields)
        ]
        for f, piece in enumerate(flux_pieces(values, 2)):
            for t in range(cells // 128):
                span_flux[t, pl.ds((f * wide + z) * tile, tile), :] = piece[:, t * 128 : t * 128 + 128]
        if source is cons_ref:
            for f, piece in enumerate(flux_pieces(values, 0)):
                stream_flux[pl.ds((f * span + at) * tile, tile), :] = piece
                current_ref[f, at] = values[f]
    band = band_ref[...]
    for f in range(fields):
        for y in range(tile):
            for t in range(cells // 128):
                lines = span_flux[t, pl.ds(f * wide * tile + y, wide, stride=tile), :]
                span_out[t, pl.ds(f * span * tile + y, span, stride=tile), :] = matmul(band, lines)
    lines = near_ref.shape[1]
    near = flux_pieces([near_ref[f] for f in range(fields)], 1)
    far = flux_pieces([far_ref[f] for f in range(fields)], 1)
    folds = 128 // span
    height = far_ref.shape[1]
    edges = []
    for f in range(fields):
        edge = matmul(matrix_ref[:, :lines], near[f])[:, halo : halo + span]
        for h in range(folds):
            low = lines + h * height
            part = matmul(matrix_ref[:, low : low + height], far[f])
            edge = edge + part[:, h * span : (h + 1) * span]
        edges.append(edge)
    weights = stream_ref[...]
    for f in range(fields):
        rows = pl.ds(f * span * tile, span * tile)
        beside = jnp.concatenate([span_out[t, rows, :] for t in range(cells // 128)], axis=1)
        total = matmul(stream_flux[rows, :], weights) + beside
        total = total.reshape(span, tile, cells)
        for z in range(span):
            term = total[z] + jnp.where(lane == 0, edges[f][:, z : z + 1], 0.0)
            partial_ref[f, z] = section_decay * reg_ref[f, z] - time_step * term


def local_part(conserved, before, after, register, near, far, matrix, band, weights):
    fields, span, rows, cells = conserved.shape
    halo = before.shape[1]
    wide = span + 2 * halo
    tile = 8
    main = pl.BlockSpec((fields, span, tile, cells), lambda i: (0, 0, i, 0))
    side = pl.BlockSpec((fields, halo, tile, cells), lambda i: (0, 0, i, 0))
    whole = lambda a: pl.BlockSpec(a.shape, lambda i: (0, 0))
    whole3 = lambda a: pl.BlockSpec(a.shape, lambda i: (0, 0, 0))
    shape = jax.ShapeDtypeStruct(conserved.shape, jnp.float32)
    return pl.pallas_call(
        functools.partial(local_kernel, halo),
        out_shape=[shape, shape],
        grid=(rows // tile,),
        in_specs=[
            main,
            side,
            side,
            main,
            pl.BlockSpec((fields, tile, near.shape[2]), lambda i: (0, i, 0)),
            whole3(near),
            whole3(far),
            pl.BlockSpec((tile, matrix.shape[1]), lambda i: (i, 0)),
            whole(band),
            whole(weights),
        ],
        out_specs=[main, main],
        scratch_shapes=[
            pltpu.VMEM((cells // 128, fields * wide * tile, 128), jnp.float32),
            pltpu.VMEM((fields * span * tile, cells), jnp.float32),
            pltpu.VMEM((cells // 128, fields * span * tile, 128), jnp.float32),
        ],
        compiler_params=pltpu.CompilerParams(vmem_limit_bytes=vmem_limit),
        cost_estimate=small_cost,
        name="local_part",
    )(conserved, before, after, register, near, near, far, matrix, band, weights)


def close_kernel(place_ref, current_ref, partial_ref, term_ref, cons_out, reg_out):
    lane = lax.broadcasted_iota(jnp.int32, term_ref.shape, 3)
    new = partial_ref[...] - time_step * jnp.where(lane == 0, 0.0, term_ref[...])
    reg_out[...] = new
    cons_out[...] = current_ref[...] + section_gain * new


def close_part(place, current, partial, term, group, offset):
    fields, part, rows, cells = term.shape
    step = math.gcd(math.gcd(part, 4), math.gcd(group, offset))
    block = (fields, step, rows, cells)
    there = pl.BlockSpec(
        block, lambda i, place: (0, (place[0] * group + offset) // step + i, 0, 0)
    )
    shape = jax.ShapeDtypeStruct(current.shape, jnp.float32)
    return pl.pallas_call(
        close_kernel,
        out_shape=[shape, shape],
        grid_spec=pltpu.PrefetchScalarGridSpec(
            num_scalar_prefetch=1,
            grid=(part // step,),
            in_specs=[there, there, pl.BlockSpec(block, lambda i, place: (0, i, 0, 0))],
            out_specs=[there, there],
        ),
        input_output_aliases={1: 0, 2: 1},
        compiler_params=pltpu.CompilerParams(vmem_limit_bytes=vmem_limit),
        cost_estimate=small_cost,
        name="close_part",
    )(place, current, partial, term)


def stream_weights(blocks):
    count, _, width, _ = blocks.shape
    lines = []
    for k in range(count):
        empty = jnp.zeros((width, width), jnp.float32)
        near = [blocks[i, 1 + k - i].T if abs(k - i) <= 1 else empty for i in range(count)]
        lines.append(jnp.concatenate(near, axis=1))
    return jnp.concatenate(lines, axis=0)


def span_band(blocks):
    count, _, width, _ = blocks.shape
    lines = []
    for k in range(count):
        line = [jnp.zeros((width, k * width), jnp.float32)] if k else []
        line += [blocks[k, j] for j in range(3)]
        line += [jnp.zeros((width, (count - 1 - k) * width), jnp.float32)] if k < count - 1 else []
        lines.append(jnp.concatenate(line, axis=1))
    return jnp.concatenate(lines, axis=0)


def local(
    conserved,
    register,
    stream_blocks,
    wall_matrix,
    span_blocks,
    inflow_gain,
    source_block,
    source_column,
):
    fields, span, rows, cells = conserved.shape
    columns = span * rows
    count = lax.axis_size("py")
    across = lax.axis_size("pz")
    row = lax.axis_index("py")
    group = span // count
    sizes = [group - group // 2, group // 2] if group >= 2 else [group]
    offsets = [sum(sizes[:c]) for c in range(len(sizes))]
    width = span_blocks.shape[2]
    steps = order_of_steps(count)
    place = lambda s: jnp.reshape((row + s) % count, (1,)).astype(jnp.int32)

    def outgoing(source, s, offset, length):
        start = ((row - s) % count) * group + offset
        return lax.dynamic_slice_in_dim(source, start, length, 1)

    received = [{} for _ in sizes]
    sent = []
    for s in steps[:-1]:
        sent.append(outgoing(after(conserved, *sent) if sent else conserved, s, 0, group))
        arrived = shift(sent[-1], "py", -s)
        for part in received:
            part[s] = arrived
    for c in range(len(sizes)):
        sent.append(outgoing(after(conserved, *sent), steps[-1], offsets[c], sizes[c]))
        piece = after(sent[-1], received[0][steps[0]]) if c else sent[-1]
        received[c][steps[-1]] = shift(piece, "py", -steps[-1])
    head, tail = after((conserved[:, :width], conserved[:, span - width :]), *sent)
    halo_after = shift(head, "pz", -1)
    halo_before = shift(tail, "pz", 1)

    place_of = lambda a: lax.dynamic_index_in_dim(
        a.reshape(count, across, columns), lax.axis_index("pz"), 1, keepdims=False
    )
    beside = lambda a, step: lax.dynamic_index_in_dim(
        lax.dynamic_index_in_dim(a.reshape(count, across, columns), row, 0, keepdims=False),
        (lax.axis_index("pz") + step) % across,
        0,
        keepdims=False,
    )
    edge_columns = width * rows

    def sources(a):
        lines = place_of(a)
        lines = lax.dynamic_slice_in_dim(jnp.concatenate([lines, lines]), row, count, 0)
        near = jnp.concatenate(
            [beside(a, -1)[columns - edge_columns :], lines[0], beside(a, 1)[:edge_columns]]
        )
        near = near.reshape(-1, rows).T
        near = jnp.pad(near, ((0, 0), (0, 128 - near.shape[1])))
        far = lines[1:].reshape(count - 1, span, rows).swapaxes(1, 2)
        far = far.reshape(128 // span, -1, span).swapaxes(0, 1)
        return near.reshape(1, -1), far.reshape(1, -1)

    block = source_block[:, :, 0]
    near_source, far_source = sources(
        ((block % across) * count + block // across) * columns + source_column
    )

    twice = jnp.concatenate([wall_matrix, wall_matrix], axis=0)
    twice = lax.dynamic_slice_in_dim(twice, row * rows, count * rows, 0)
    twice = jnp.concatenate([twice, twice], axis=1)
    matrix = lax.dynamic_slice_in_dim(twice, row * rows, count * rows, 1)

    local_blocks = span // width
    own_blocks = lax.dynamic_slice_in_dim(
        span_blocks, lax.axis_index("pz") * local_blocks, local_blocks, 0
    )
    band = span_band(own_blocks)
    weights = stream_weights(stream_blocks)
    small = [matrix, band, weights, near_source, far_source]

    recycle = after(conserved, head, tail, *small)[:, :, :, 3 * cells // 4].reshape(-1, 128)
    along = lax.all_to_all(
        jnp.broadcast_to(recycle, (count,) + recycle.shape), "py", split_axis=0, concat_axis=0
    )

    along = after(along, *received[0].values())
    prepared = [band, weights, near_source, far_source, halo_after, halo_before]

    def wall(c, *earlier):
        return wall_part(
            place(0),
            conserved,
            [received[c][s] for s in range(1, count)],
            after(matrix, *earlier),
            offsets[c],
            sizes[c],
        )

    returned = [{} for _ in sizes]

    def give(c, pieces, *earlier):
        returned[c][0] = pieces[0]
        for s in steps:
            returned[c][s] = shift(after(pieces[s], *earlier), "py", s)

    walls = [wall(0, *prepared)]
    give(0, walls[0])

    table = lax.all_gather(along, "pz", axis=0).reshape(across * count, fields, -1, 128)
    near = inlet_part(table, after(near_source, walls[0][0]), inflow_gain)
    far = inlet_part(table, after(far_source, near), inflow_gain)
    current, partial = local_part(
        conserved,
        halo_before,
        halo_after,
        register,
        near,
        far,
        matrix,
        band,
        weights,
    )
    for c in range(1, len(sizes)):
        walls.append(wall(c, far))
        give(c, walls[c])
    for c in range(len(sizes)):
        for s in [0] + steps:
            current, partial = close_part(
                place(-s), current, partial, returned[c][s], group, offsets[c]
            )
    return (current, partial)


def solution(mesh):
    return jax.shard_map(
        local,
        mesh=mesh,
        in_specs=(
            P(None, "pz", "py", None),
            P(None, "pz", "py", None),
            P(),
            P(),
            P(),
            P(),
            P(),
            P(),
        ),
        out_specs=(P(None, "pz", "py", None), P(None, "pz", "py", None)),
        check_vma=False,
    )
```

```python
import functools
import math

import jax
import jax.numpy as jnp
from jax import lax
from jax.experimental import pallas as pl
from jax.experimental.pallas import tpu as pltpu
from jax.sharding import PartitionSpec as P

highest = lax.Precision.HIGHEST
section_decay = -5.0 / 9.0
section_gain = 15.0 / 16.0
time_step = 0.1
vmem_limit = 48 * 1024 * 1024
small_cost = pl.CostEstimate(flops=1, bytes_accessed=1, transcendentals=0)


def shift(values, axis, step):
    count = lax.axis_size(axis)
    return lax.ppermute(values, axis, [(i, (i + step) % count) for i in range(count)])


def after(values, *earlier):
    return lax.optimization_barrier((values, earlier))[0]


def order_of_steps(count):
    pairs = [(s, count - s) for s in range(1, (count + 1) // 2)]
    middle = [count // 2] if count % 2 == 0 and count > 1 else []
    return [s for pair in pairs for s in pair] + middle


def flux_pieces(values, direction):
    inverse = 1.0 / values[0]
    speeds = [values[1 + d] * inverse for d in range(3)]
    pressure = 0.4 * (
        values[4] - 0.5 * (values[1] * speeds[0] + values[2] * speeds[1] + values[3] * speeds[2])
    )
    velocity = speeds[direction]
    pieces = [values[1 + direction]]
    for component in range(1, 4):
        moment = values[component] * velocity
        if component - 1 == direction:
            moment = moment + pressure
        pieces.append(moment)
    pieces.append((values[4] + pressure) * velocity)
    return pieces


def matmul(a, b):
    return jnp.dot(a, b, precision=highest, preferred_element_type=jnp.float32)


def wall_kernel(count, fields, place_ref, own_ref, *refs):
    received = refs[: count - 1]
    matrix_ref = refs[count - 1]
    outs = refs[count:]
    rows, cells = own_ref.shape[2:]
    sources = [own_ref] + list(received)
    lines = []
    for source in sources:
        lines.append(
            jnp.concatenate(flux_pieces([source[f, 0] for f in range(fields)], 1), axis=1)
        )
    term = matmul(matrix_ref[...], jnp.concatenate(lines, axis=0))
    for s, out in enumerate(outs):
        for f in range(fields):
            out[f, 0] = term[s * rows : (s + 1) * rows, f * cells : (f + 1) * cells]


def wall_part(place, conserved, received, matrix, offset, part):
    fields, span, rows, cells = conserved.shape
    count = len(received) + 1
    group = span // count
    block = (fields, 1, rows, cells)
    piece = pl.BlockSpec(block, lambda i, place: (0, i, 0, 0))
    within = lambda a: piece if a.shape[1] == part else whole
    whole = pl.BlockSpec(block, lambda i, place: (0, offset + i, 0, 0))
    return pl.pallas_call(
        functools.partial(wall_kernel, count, fields),
        out_shape=[jax.ShapeDtypeStruct((fields, part, rows, cells), jnp.float32)] * count,
        grid_spec=pltpu.PrefetchScalarGridSpec(
            num_scalar_prefetch=1,
            grid=(part,),
            in_specs=[pl.BlockSpec(block, lambda i, place: (0, place[0] * group + offset + i, 0, 0))]
            + [within(a) for a in received]
            + [pl.BlockSpec(matrix.shape, lambda i, place: (0, 0))],
            out_specs=[piece] * count,
        ),
        compiler_params=pltpu.CompilerParams(vmem_limit_bytes=vmem_limit),
        cost_estimate=small_cost,
        name="wall_part",
    )(place, conserved, *received, matrix)


def inlet_kernel(table_ref, source_ref, gain_ref, out_ref, split):
    slots, fields, lines, lanes = table_ref.shape
    height = slots * lines

    @pl.when(pl.program_id(0) == 0)
    def _():
        for f in range(fields):
            rest = table_ref[:, f].reshape(height, lanes)
            for k in range(3):
                piece = rest.astype(jnp.bfloat16)
                split[pl.ds((k * fields + f) * lanes, lanes), :] = piece.T
                rest = rest - piece.astype(jnp.float32)

    width = source_ref.shape[1]
    source = source_ref[...]
    line = source // lanes
    choice = jnp.where(
        lax.broadcasted_iota(jnp.int32, (height, width), 0) == line, 1.0, 0.0
    ).astype(jnp.bfloat16)
    lane = lax.broadcasted_iota(jnp.int32, (lanes, width), 0) == source % lanes
    found = jnp.dot(split[...], choice, preferred_element_type=jnp.float32)
    found = found.reshape(3, fields, lanes, width)
    for f in range(fields):
        total = found[2, f] + found[1, f] + found[0, f]
        picked = jnp.sum(jnp.where(lane, total, 0.0), axis=0, keepdims=True)
        picked = picked * gain_ref[f]
        for k in range(width // lanes):
            out_ref[f, k : k + 1, :] = picked[:, k * lanes : (k + 1) * lanes]


def inlet_part(table, source, gain):
    slots, fields, lines, lanes = table.shape
    height = slots * lines
    columns = source.shape[1]
    width = 8 * lanes
    row = pl.BlockSpec((1, width), lambda i: (0, i))
    return pl.pallas_call(
        inlet_kernel,
        out_shape=jax.ShapeDtypeStruct((fields, columns // lanes, lanes), jnp.float32),
        grid=(columns // width,),
        in_specs=[
            pl.BlockSpec(table.shape, lambda i: (0, 0, 0, 0)),
            row,
            pl.BlockSpec(memory_space=pltpu.SMEM),
        ],
        out_specs=pl.BlockSpec((fields, 8, lanes), lambda i: (0, i, 0)),
        scratch_shapes=[pltpu.VMEM((3 * fields * lanes, height), jnp.bfloat16)],
        compiler_params=pltpu.CompilerParams(vmem_limit_bytes=vmem_limit),
        cost_estimate=small_cost,
        name="inlet_part",
    )(table, source, gain)


def local_kernel(
    halo,
    cons_ref,
    before_ref,
    after_ref,
    reg_ref,
    inlet_ref,
    near_ref,
    far_ref,
    matrix_ref,
    band_ref,
    stream_ref,
    current_ref,
    partial_ref,
    span_flux,
    stream_flux,
    span_out,
):
    fields, span, tile, cells = cons_ref.shape
    wide = span + 2 * halo
    lane = lax.broadcasted_iota(jnp.int32, (tile, cells), 1)
    for z in range(wide):
        if z < halo:
            source, at = before_ref, z
        elif z < halo + span:
            source, at = cons_ref, z - halo
        else:
            source, at = after_ref, z - halo - span
        values = [
            jnp.where(lane == 0, inlet_ref[f, :, z : z + 1], source[f, at]) for f in range(fields)
        ]
        for f, piece in enumerate(flux_pieces(values, 2)):
            for t in range(cells // 128):
                span_flux[t, pl.ds((f * wide + z) * tile, tile), :] = piece[:, t * 128 : t * 128 + 128]
        if source is cons_ref:
            for f, piece in enumerate(flux_pieces(values, 0)):
                stream_flux[pl.ds((f * span + at) * tile, tile), :] = piece
                current_ref[f, at] = values[f]
    band = band_ref[...]
    for f in range(fields):
        for y in range(tile):
            for t in range(cells // 128):
                lines = span_flux[t, pl.ds(f * wide * tile + y, wide, stride=tile), :]
                span_out[t, pl.ds(f * span * tile + y, span, stride=tile), :] = matmul(band, lines)
    lines = near_ref.shape[1]
    near = flux_pieces([near_ref[f] for f in range(fields)], 1)
    far = flux_pieces([far_ref[f] for f in range(fields)], 1)
    folds = 128 // span
    height = far_ref.shape[1]
    edges = []
    for f in range(fields):
        edge = matmul(matrix_ref[:, :lines], near[f])[:, halo : halo + span]
        for h in range(folds):
            low = lines + h * height
            part = matmul(matrix_ref[:, low : low + height], far[f])
            edge = edge + part[:, h * span : (h + 1) * span]
        edges.append(edge)
    weights = stream_ref[...]
    for f in range(fields):
        rows = pl.ds(f * span * tile, span * tile)
        beside = jnp.concatenate([span_out[t, rows, :] for t in range(cells // 128)], axis=1)
        total = matmul(stream_flux[rows, :], weights) + beside
        total = total.reshape(span, tile, cells)
        for z in range(span):
            term = total[z] + jnp.where(lane == 0, edges[f][:, z : z + 1], 0.0)
            partial_ref[f, z] = section_decay * reg_ref[f, z] - time_step * term


def local_part(conserved, before, after, register, near, far, matrix, band, weights):
    fields, span, rows, cells = conserved.shape
    halo = before.shape[1]
    wide = span + 2 * halo
    tile = 8
    main = pl.BlockSpec((fields, span, tile, cells), lambda i: (0, 0, i, 0))
    side = pl.BlockSpec((fields, halo, tile, cells), lambda i: (0, 0, i, 0))
    whole = lambda a: pl.BlockSpec(a.shape, lambda i: (0, 0))
    whole3 = lambda a: pl.BlockSpec(a.shape, lambda i: (0, 0, 0))
    shape = jax.ShapeDtypeStruct(conserved.shape, jnp.float32)
    return pl.pallas_call(
        functools.partial(local_kernel, halo),
        out_shape=[shape, shape],
        grid=(rows // tile,),
        in_specs=[
            main,
            side,
            side,
            main,
            pl.BlockSpec((fields, tile, near.shape[2]), lambda i: (0, i, 0)),
            whole3(near),
            whole3(far),
            pl.BlockSpec((tile, matrix.shape[1]), lambda i: (i, 0)),
            whole(band),
            whole(weights),
        ],
        out_specs=[main, main],
        scratch_shapes=[
            pltpu.VMEM((cells // 128, fields * wide * tile, 128), jnp.float32),
            pltpu.VMEM((fields * span * tile, cells), jnp.float32),
            pltpu.VMEM((cells // 128, fields * span * tile, 128), jnp.float32),
        ],
        compiler_params=pltpu.CompilerParams(vmem_limit_bytes=vmem_limit),
        cost_estimate=small_cost,
        name="local_part",
    )(conserved, before, after, register, near, near, far, matrix, band, weights)


def close_kernel(place_ref, current_ref, partial_ref, term_ref, cons_out, reg_out):
    lane = lax.broadcasted_iota(jnp.int32, term_ref.shape, 3)
    new = partial_ref[...] - time_step * jnp.where(lane == 0, 0.0, term_ref[...])
    reg_out[...] = new
    cons_out[...] = current_ref[...] + section_gain * new


def close_part(place, current, partial, term, group, offset):
    fields, part, rows, cells = term.shape
    step = math.gcd(math.gcd(part, 4), math.gcd(group, offset))
    block = (fields, step, rows, cells)
    there = pl.BlockSpec(
        block, lambda i, place: (0, (place[0] * group + offset) // step + i, 0, 0)
    )
    shape = jax.ShapeDtypeStruct(current.shape, jnp.float32)
    return pl.pallas_call(
        close_kernel,
        out_shape=[shape, shape],
        grid_spec=pltpu.PrefetchScalarGridSpec(
            num_scalar_prefetch=1,
            grid=(part // step,),
            in_specs=[there, there, pl.BlockSpec(block, lambda i, place: (0, i, 0, 0))],
            out_specs=[there, there],
        ),
        input_output_aliases={1: 0, 2: 1},
        compiler_params=pltpu.CompilerParams(vmem_limit_bytes=vmem_limit),
        cost_estimate=small_cost,
        name="close_part",
    )(place, current, partial, term)


def stream_weights(blocks):
    count, _, width, _ = blocks.shape
    lines = []
    for k in range(count):
        empty = jnp.zeros((width, width), jnp.float32)
        near = [blocks[i, 1 + k - i].T if abs(k - i) <= 1 else empty for i in range(count)]
        lines.append(jnp.concatenate(near, axis=1))
    return jnp.concatenate(lines, axis=0)


def span_band(blocks):
    count, _, width, _ = blocks.shape
    lines = []
    for k in range(count):
        line = [jnp.zeros((width, k * width), jnp.float32)] if k else []
        line += [blocks[k, j] for j in range(3)]
        line += [jnp.zeros((width, (count - 1 - k) * width), jnp.float32)] if k < count - 1 else []
        lines.append(jnp.concatenate(line, axis=1))
    return jnp.concatenate(lines, axis=0)


def local(
    conserved,
    register,
    stream_blocks,
    wall_matrix,
    span_blocks,
    inflow_gain,
    source_block,
    source_column,
):
    fields, span, rows, cells = conserved.shape
    columns = span * rows
    count = lax.axis_size("py")
    across = lax.axis_size("pz")
    row = lax.axis_index("py")
    group = span // count
    sizes = [group - group // 2, group // 2] if group >= 2 else [group]
    offsets = [sum(sizes[:c]) for c in range(len(sizes))]
    width = span_blocks.shape[2]
    steps = order_of_steps(count)
    place = lambda s: jnp.reshape((row + s) % count, (1,)).astype(jnp.int32)

    def outgoing(source, s, offset, length):
        start = ((row - s) % count) * group + offset
        return lax.dynamic_slice_in_dim(source, start, length, 1)

    received = [{} for _ in sizes]
    sent = [outgoing(conserved, steps[-1], 0, sizes[0])]
    received[0][steps[-1]] = shift(sent[0], "py", -steps[-1])
    for s in steps[:-1]:
        sent.append(outgoing(after(conserved, *sent), s, 0, group))
        arrived = shift(sent[-1], "py", -s)
        for part in received:
            part[s] = arrived
    for c in range(1, len(sizes)):
        sent.append(outgoing(after(conserved, *sent), steps[-1], offsets[c], sizes[c]))
        piece = after(sent[-1], received[0][steps[0]])
        received[c][steps[-1]] = shift(piece, "py", -steps[-1])
    head, tail = after((conserved[:, :width], conserved[:, span - width :]), *sent)
    halo_after = shift(head, "pz", -1)
    halo_before = shift(tail, "pz", 1)

    place_of = lambda a: lax.dynamic_index_in_dim(
        a.reshape(count, across, columns), lax.axis_index("pz"), 1, keepdims=False
    )
    beside = lambda a, step: lax.dynamic_index_in_dim(
        lax.dynamic_index_in_dim(a.reshape(count, across, columns), row, 0, keepdims=False),
        (lax.axis_index("pz") + step) % across,
        0,
        keepdims=False,
    )
    edge_columns = width * rows

    def sources(a):
        lines = place_of(a)
        lines = lax.dynamic_slice_in_dim(jnp.concatenate([lines, lines]), row, count, 0)
        near = jnp.concatenate(
            [beside(a, -1)[columns - edge_columns :], lines[0], beside(a, 1)[:edge_columns]]
        )
        near = near.reshape(-1, rows).T
        near = jnp.pad(near, ((0, 0), (0, 128 - near.shape[1])))
        far = lines[1:].reshape(count - 1, span, rows).swapaxes(1, 2)
        far = far.reshape(128 // span, -1, span).swapaxes(0, 1)
        return near.reshape(1, -1), far.reshape(1, -1)

    block = source_block[:, :, 0]
    near_source, far_source = sources(
        ((block % across) * count + block // across) * columns + source_column
    )

    twice = jnp.concatenate([wall_matrix, wall_matrix], axis=0)
    twice = lax.dynamic_slice_in_dim(twice, row * rows, count * rows, 0)
    twice = jnp.concatenate([twice, twice], axis=1)
    matrix = lax.dynamic_slice_in_dim(twice, row * rows, count * rows, 1)

    local_blocks = span // width
    own_blocks = lax.dynamic_slice_in_dim(
        span_blocks, lax.axis_index("pz") * local_blocks, local_blocks, 0
    )
    band = span_band(own_blocks)
    weights = stream_weights(stream_blocks)
    small = [matrix, band, weights, near_source, far_source]

    recycle = after(conserved, head, tail, *small)[:, :, :, 3 * cells // 4].reshape(-1, 128)
    along = lax.all_to_all(
        jnp.broadcast_to(recycle, (count,) + recycle.shape), "py", split_axis=0, concat_axis=0
    )

    along = after(along, *received[0].values())
    prepared = [band, weights, near_source, far_source, halo_after, halo_before]

    def wall(c, *earlier):
        return wall_part(
            place(0),
            conserved,
            [received[c][s] for s in range(1, count)],
            after(matrix, *earlier),
            offsets[c],
            sizes[c],
        )

    returned = [{} for _ in sizes]

    def give(c, pieces, *earlier):
        returned[c][0] = pieces[0]
        for s in steps:
            returned[c][s] = shift(after(pieces[s], *earlier), "py", s)

    walls = [wall(0, *prepared)]
    give(0, walls[0])

    table = lax.all_gather(along, "pz", axis=0).reshape(across * count, fields, -1, 128)
    near = inlet_part(table, after(near_source, walls[0][0]), inflow_gain)
    far = inlet_part(table, after(far_source, near), inflow_gain)
    current, partial = local_part(
        conserved,
        halo_before,
        halo_after,
        register,
        near,
        far,
        matrix,
        band,
        weights,
    )
    for c in range(1, len(sizes)):
        walls.append(wall(c, far))
        give(c, walls[c])
    for c in range(len(sizes)):
        for s in [0] + steps:
            current, partial = close_part(
                place(-s), current, partial, returned[c][s], group, offsets[c]
            )
    return (current, partial)


def solution(mesh):
    return jax.shard_map(
        local,
        mesh=mesh,
        in_specs=(
            P(None, "pz", "py", None),
            P(None, "pz", "py", None),
            P(),
            P(),
            P(),
            P(),
            P(),
            P(),
        ),
        out_specs=(P(None, "pz", "py", None), P(None, "pz", "py", None)),
        check_vma=False,
    )
```

```python
import functools
import math

import jax
import jax.numpy as jnp
from jax import lax
from jax.experimental import pallas as pl
from jax.experimental.pallas import tpu as pltpu
from jax.sharding import PartitionSpec as P

highest = lax.Precision.HIGHEST
section_decay = -5.0 / 9.0
section_gain = 15.0 / 16.0
time_step = 0.1
vmem_limit = 48 * 1024 * 1024
small_cost = pl.CostEstimate(flops=1, bytes_accessed=1, transcendentals=0)


def shift(values, axis, step):
    count = lax.axis_size(axis)
    return lax.ppermute(values, axis, [(i, (i + step) % count) for i in range(count)])


def after(values, *earlier):
    return lax.optimization_barrier((values, earlier))[0]


def order_of_steps(count):
    pairs = [(s, count - s) for s in range(1, (count + 1) // 2)]
    middle = [count // 2] if count % 2 == 0 and count > 1 else []
    return [s for pair in pairs for s in pair] + middle


def flux_pieces(values, direction):
    inverse = 1.0 / values[0]
    speeds = [values[1 + d] * inverse for d in range(3)]
    pressure = 0.4 * (
        values[4] - 0.5 * (values[1] * speeds[0] + values[2] * speeds[1] + values[3] * speeds[2])
    )
    velocity = speeds[direction]
    pieces = [values[1 + direction]]
    for component in range(1, 4):
        moment = values[component] * velocity
        if component - 1 == direction:
            moment = moment + pressure
        pieces.append(moment)
    pieces.append((values[4] + pressure) * velocity)
    return pieces


def matmul(a, b):
    return jnp.dot(a, b, precision=highest, preferred_element_type=jnp.float32)


def wall_kernel(count, fields, place_ref, own_ref, *refs):
    received = refs[: count - 1]
    matrix_ref = refs[count - 1]
    outs = refs[count:]
    rows, cells = own_ref.shape[2:]
    sources = [own_ref] + list(received)
    lines = []
    for source in sources:
        lines.append(
            jnp.concatenate(flux_pieces([source[f, 0] for f in range(fields)], 1), axis=1)
        )
    term = matmul(matrix_ref[...], jnp.concatenate(lines, axis=0))
    for s, out in enumerate(outs):
        for f in range(fields):
            out[f, 0] = term[s * rows : (s + 1) * rows, f * cells : (f + 1) * cells]


def wall_part(place, conserved, received, matrix, offset, part):
    fields, span, rows, cells = conserved.shape
    count = len(received) + 1
    group = span // count
    block = (fields, 1, rows, cells)
    piece = pl.BlockSpec(block, lambda i, place: (0, i, 0, 0))
    within = lambda a: piece if a.shape[1] == part else whole
    whole = pl.BlockSpec(block, lambda i, place: (0, offset + i, 0, 0))
    return pl.pallas_call(
        functools.partial(wall_kernel, count, fields),
        out_shape=[jax.ShapeDtypeStruct((fields, part, rows, cells), jnp.float32)] * count,
        grid_spec=pltpu.PrefetchScalarGridSpec(
            num_scalar_prefetch=1,
            grid=(part,),
            in_specs=[pl.BlockSpec(block, lambda i, place: (0, place[0] * group + offset + i, 0, 0))]
            + [within(a) for a in received]
            + [pl.BlockSpec(matrix.shape, lambda i, place: (0, 0))],
            out_specs=[piece] * count,
        ),
        compiler_params=pltpu.CompilerParams(vmem_limit_bytes=vmem_limit),
        cost_estimate=small_cost,
        name="wall_part",
    )(place, conserved, *received, matrix)


def inlet_kernel(table_ref, source_ref, gain_ref, out_ref, split):
    slots, fields, lines, lanes = table_ref.shape
    height = slots * lines

    @pl.when(pl.program_id(0) == 0)
    def _():
        for f in range(fields):
            rest = table_ref[:, f].reshape(height, lanes)
            for k in range(3):
                piece = rest.astype(jnp.bfloat16)
                split[pl.ds((k * fields + f) * lanes, lanes), :] = piece.T
                rest = rest - piece.astype(jnp.float32)

    width = source_ref.shape[1]
    source = source_ref[...]
    line = source // lanes
    choice = jnp.where(
        lax.broadcasted_iota(jnp.int32, (height, width), 0) == line, 1.0, 0.0
    ).astype(jnp.bfloat16)
    lane = lax.broadcasted_iota(jnp.int32, (lanes, width), 0) == source % lanes
    found = jnp.dot(split[...], choice, preferred_element_type=jnp.float32)
    found = found.reshape(3, fields, lanes, width)
    for f in range(fields):
        total = found[2, f] + found[1, f] + found[0, f]
        picked = jnp.sum(jnp.where(lane, total, 0.0), axis=0, keepdims=True)
        picked = picked * gain_ref[f]
        for k in range(width // lanes):
            out_ref[f, k : k + 1, :] = picked[:, k * lanes : (k + 1) * lanes]


def inlet_part(table, source, gain):
    slots, fields, lines, lanes = table.shape
    height = slots * lines
    columns = source.shape[1]
    width = 8 * lanes
    row = pl.BlockSpec((1, width), lambda i: (0, i))
    return pl.pallas_call(
        inlet_kernel,
        out_shape=jax.ShapeDtypeStruct((fields, columns // lanes, lanes), jnp.float32),
        grid=(columns // width,),
        in_specs=[
            pl.BlockSpec(table.shape, lambda i: (0, 0, 0, 0)),
            row,
            pl.BlockSpec(memory_space=pltpu.SMEM),
        ],
        out_specs=pl.BlockSpec((fields, 8, lanes), lambda i: (0, i, 0)),
        scratch_shapes=[pltpu.VMEM((3 * fields * lanes, height), jnp.bfloat16)],
        compiler_params=pltpu.CompilerParams(vmem_limit_bytes=vmem_limit),
        cost_estimate=small_cost,
        name="inlet_part",
    )(table, source, gain)


def local_kernel(
    halo,
    cons_ref,
    before_ref,
    after_ref,
    reg_ref,
    inlet_ref,
    near_ref,
    far_ref,
    matrix_ref,
    band_ref,
    stream_ref,
    current_ref,
    partial_ref,
    span_flux,
    stream_flux,
    span_out,
):
    fields, span, tile, cells = cons_ref.shape
    wide = span + 2 * halo
    lane = lax.broadcasted_iota(jnp.int32, (tile, cells), 1)
    for z in range(wide):
        if z < halo:
            source, at = before_ref, z
        elif z < halo + span:
            source, at = cons_ref, z - halo
        else:
            source, at = after_ref, z - halo - span
        values = [
            jnp.where(lane == 0, inlet_ref[f, :, z : z + 1], source[f, at]) for f in range(fields)
        ]
        for f, piece in enumerate(flux_pieces(values, 2)):
            for t in range(cells // 128):
                span_flux[t, pl.ds((f * wide + z) * tile, tile), :] = piece[:, t * 128 : t * 128 + 128]
        if source is cons_ref:
            for f, piece in enumerate(flux_pieces(values, 0)):
                stream_flux[pl.ds((f * span + at) * tile, tile), :] = piece
                current_ref[f, at] = values[f]
    band = band_ref[...]
    for f in range(fields):
        for y in range(tile):
            for t in range(cells // 128):
                lines = span_flux[t, pl.ds(f * wide * tile + y, wide, stride=tile), :]
                span_out[t, pl.ds(f * span * tile + y, span, stride=tile), :] = matmul(band, lines)
    lines = near_ref.shape[1]
    near = flux_pieces([near_ref[f] for f in range(fields)], 1)
    far = flux_pieces([far_ref[f] for f in range(fields)], 1)
    folds = 128 // span
    height = far_ref.shape[1]
    edges = []
    for f in range(fields):
        edge = matmul(matrix_ref[:, :lines], near[f])[:, halo : halo + span]
        for h in range(folds):
            low = lines + h * height
            part = matmul(matrix_ref[:, low : low + height], far[f])
            edge = edge + part[:, h * span : (h + 1) * span]
        edges.append(edge)
    weights = stream_ref[...]
    for f in range(fields):
        rows = pl.ds(f * span * tile, span * tile)
        beside = jnp.concatenate([span_out[t, rows, :] for t in range(cells // 128)], axis=1)
        total = matmul(stream_flux[rows, :], weights) + beside
        total = total.reshape(span, tile, cells)
        for z in range(span):
            term = total[z] + jnp.where(lane == 0, edges[f][:, z : z + 1], 0.0)
            partial_ref[f, z] = section_decay * reg_ref[f, z] - time_step * term


def local_part(conserved, before, after, register, near, far, matrix, band, weights):
    fields, span, rows, cells = conserved.shape
    halo = before.shape[1]
    wide = span + 2 * halo
    tile = 8
    main = pl.BlockSpec((fields, span, tile, cells), lambda i: (0, 0, i, 0))
    side = pl.BlockSpec((fields, halo, tile, cells), lambda i: (0, 0, i, 0))
    whole = lambda a: pl.BlockSpec(a.shape, lambda i: (0, 0))
    whole3 = lambda a: pl.BlockSpec(a.shape, lambda i: (0, 0, 0))
    shape = jax.ShapeDtypeStruct(conserved.shape, jnp.float32)
    return pl.pallas_call(
        functools.partial(local_kernel, halo),
        out_shape=[shape, shape],
        grid=(rows // tile,),
        in_specs=[
            main,
            side,
            side,
            main,
            pl.BlockSpec((fields, tile, near.shape[2]), lambda i: (0, i, 0)),
            whole3(near),
            whole3(far),
            pl.BlockSpec((tile, matrix.shape[1]), lambda i: (i, 0)),
            whole(band),
            whole(weights),
        ],
        out_specs=[main, main],
        scratch_shapes=[
            pltpu.VMEM((cells // 128, fields * wide * tile + tile, 128), jnp.float32),
            pltpu.VMEM((fields * span * tile, cells), jnp.float32),
            pltpu.VMEM((cells // 128, fields * span * tile + tile, 128), jnp.float32),
        ],
        compiler_params=pltpu.CompilerParams(vmem_limit_bytes=vmem_limit),
        cost_estimate=small_cost,
        name="local_part",
    )(conserved, before, after, register, near, near, far, matrix, band, weights)


def close_kernel(place_ref, current_ref, partial_ref, term_ref, cons_out, reg_out):
    lane = lax.broadcasted_iota(jnp.int32, term_ref.shape, 3)
    new = partial_ref[...] - time_step * jnp.where(lane == 0, 0.0, term_ref[...])
    reg_out[...] = new
    cons_out[...] = current_ref[...] + section_gain * new


def close_part(place, current, partial, term, group, offset):
    fields, part, rows, cells = term.shape
    step = math.gcd(math.gcd(part, 4), math.gcd(group, offset))
    block = (fields, step, rows, cells)
    there = pl.BlockSpec(
        block, lambda i, place: (0, (place[0] * group + offset) // step + i, 0, 0)
    )
    shape = jax.ShapeDtypeStruct(current.shape, jnp.float32)
    return pl.pallas_call(
        close_kernel,
        out_shape=[shape, shape],
        grid_spec=pltpu.PrefetchScalarGridSpec(
            num_scalar_prefetch=1,
            grid=(part // step,),
            in_specs=[there, there, pl.BlockSpec(block, lambda i, place: (0, i, 0, 0))],
            out_specs=[there, there],
        ),
        input_output_aliases={1: 0, 2: 1},
        compiler_params=pltpu.CompilerParams(vmem_limit_bytes=vmem_limit),
        cost_estimate=small_cost,
        name="close_part",
    )(place, current, partial, term)


def stream_weights(blocks):
    count, _, width, _ = blocks.shape
    lines = []
    for k in range(count):
        empty = jnp.zeros((width, width), jnp.float32)
        near = [blocks[i, 1 + k - i].T if abs(k - i) <= 1 else empty for i in range(count)]
        lines.append(jnp.concatenate(near, axis=1))
    return jnp.concatenate(lines, axis=0)


def span_band(blocks):
    count, _, width, _ = blocks.shape
    lines = []
    for k in range(count):
        line = [jnp.zeros((width, k * width), jnp.float32)] if k else []
        line += [blocks[k, j] for j in range(3)]
        line += [jnp.zeros((width, (count - 1 - k) * width), jnp.float32)] if k < count - 1 else []
        lines.append(jnp.concatenate(line, axis=1))
    return jnp.concatenate(lines, axis=0)


def local(
    conserved,
    register,
    stream_blocks,
    wall_matrix,
    span_blocks,
    inflow_gain,
    source_block,
    source_column,
):
    fields, span, rows, cells = conserved.shape
    columns = span * rows
    count = lax.axis_size("py")
    across = lax.axis_size("pz")
    row = lax.axis_index("py")
    group = span // count
    sizes = [group - group // 2, group // 2] if group >= 2 else [group]
    offsets = [sum(sizes[:c]) for c in range(len(sizes))]
    width = span_blocks.shape[2]
    steps = order_of_steps(count)
    place = lambda s: jnp.reshape((row + s) % count, (1,)).astype(jnp.int32)

    def outgoing(source, s, offset, length):
        start = ((row - s) % count) * group + offset
        return lax.dynamic_slice_in_dim(source, start, length, 1)

    received = [{} for _ in sizes]
    sent = [outgoing(conserved, steps[-1], 0, sizes[0])]
    received[0][steps[-1]] = shift(sent[0], "py", -steps[-1])
    for s in steps[:-1]:
        sent.append(outgoing(after(conserved, *sent), s, 0, group))
        arrived = shift(sent[-1], "py", -s)
        for part in received:
            part[s] = arrived
    for c in range(1, len(sizes)):
        sent.append(outgoing(after(conserved, *sent), steps[-1], offsets[c], sizes[c]))
        piece = after(sent[-1], received[0][steps[0]])
        received[c][steps[-1]] = shift(piece, "py", -steps[-1])
    head, tail = after((conserved[:, :width], conserved[:, span - width :]), *sent)
    halo_after = shift(head, "pz", -1)
    halo_before = shift(tail, "pz", 1)

    place_of = lambda a: lax.dynamic_index_in_dim(
        a.reshape(count, across, columns), lax.axis_index("pz"), 1, keepdims=False
    )
    beside = lambda a, step: lax.dynamic_index_in_dim(
        lax.dynamic_index_in_dim(a.reshape(count, across, columns), row, 0, keepdims=False),
        (lax.axis_index("pz") + step) % across,
        0,
        keepdims=False,
    )
    edge_columns = width * rows

    def sources(a):
        lines = place_of(a)
        lines = lax.dynamic_slice_in_dim(jnp.concatenate([lines, lines]), row, count, 0)
        near = jnp.concatenate(
            [beside(a, -1)[columns - edge_columns :], lines[0], beside(a, 1)[:edge_columns]]
        )
        near = near.reshape(-1, rows).T
        near = jnp.pad(near, ((0, 0), (0, 128 - near.shape[1])))
        far = lines[1:].reshape(count - 1, span, rows).swapaxes(1, 2)
        far = far.reshape(128 // span, -1, span).swapaxes(0, 1)
        return near.reshape(1, -1), far.reshape(1, -1)

    block = source_block[:, :, 0]
    near_source, far_source = sources(
        ((block % across) * count + block // across) * columns + source_column
    )

    twice = jnp.concatenate([wall_matrix, wall_matrix], axis=0)
    twice = lax.dynamic_slice_in_dim(twice, row * rows, count * rows, 0)
    twice = jnp.concatenate([twice, twice], axis=1)
    matrix = lax.dynamic_slice_in_dim(twice, row * rows, count * rows, 1)

    local_blocks = span // width
    own_blocks = lax.dynamic_slice_in_dim(
        span_blocks, lax.axis_index("pz") * local_blocks, local_blocks, 0
    )
    band = span_band(own_blocks)
    weights = stream_weights(stream_blocks)
    small = [matrix, band, weights, near_source, far_source]

    recycle = after(conserved, head, tail, *small)[:, :, :, 3 * cells // 4].reshape(-1, 128)
    along = lax.all_to_all(
        jnp.broadcast_to(recycle, (count,) + recycle.shape), "py", split_axis=0, concat_axis=0
    )

    along = after(along, *received[0].values())
    prepared = [band, weights, near_source, far_source, halo_after, halo_before]

    def wall(c, *earlier):
        return wall_part(
            place(0),
            conserved,
            [received[c][s] for s in range(1, count)],
            after(matrix, *earlier),
            offsets[c],
            sizes[c],
        )

    returned = [{} for _ in sizes]

    def give(c, pieces, *earlier):
        returned[c][0] = pieces[0]
        for s in steps:
            returned[c][s] = shift(after(pieces[s], *earlier), "py", s)

    walls = [wall(0, *prepared)]
    give(0, walls[0])

    table = lax.all_gather(along, "pz", axis=0).reshape(across * count, fields, -1, 128)
    near = inlet_part(table, after(near_source, walls[0][0]), inflow_gain)
    far = inlet_part(table, after(far_source, near), inflow_gain)
    current, partial = local_part(
        conserved,
        halo_before,
        halo_after,
        register,
        near,
        far,
        matrix,
        band,
        weights,
    )
    for c in range(1, len(sizes)):
        walls.append(wall(c, far))
        give(c, walls[c])
    for c in range(len(sizes)):
        for s in [0] + steps:
            current, partial = close_part(
                place(-s), current, partial, returned[c][s], group, offsets[c]
            )
    return (current, partial)


def solution(mesh):
    return jax.shard_map(
        local,
        mesh=mesh,
        in_specs=(
            P(None, "pz", "py", None),
            P(None, "pz", "py", None),
            P(),
            P(),
            P(),
            P(),
            P(),
            P(),
        ),
        out_specs=(P(None, "pz", "py", None), P(None, "pz", "py", None)),
        check_vma=False,
    )
```

```python
import functools
import math

import jax
import jax.numpy as jnp
from jax import lax
from jax.experimental import pallas as pl
from jax.experimental.pallas import tpu as pltpu
from jax.sharding import PartitionSpec as P

highest = lax.Precision.HIGHEST
section_decay = -5.0 / 9.0
section_gain = 15.0 / 16.0
time_step = 0.1
vmem_limit = 48 * 1024 * 1024
small_cost = pl.CostEstimate(flops=1, bytes_accessed=1, transcendentals=0)


def shift(values, axis, step):
    count = lax.axis_size(axis)
    return lax.ppermute(values, axis, [(i, (i + step) % count) for i in range(count)])


def after(values, *earlier):
    return lax.optimization_barrier((values, earlier))[0]


def order_of_steps(count):
    pairs = [(s, count - s) for s in range(1, (count + 1) // 2)]
    middle = [count // 2] if count % 2 == 0 and count > 1 else []
    return [s for pair in pairs for s in pair] + middle


def flux_pieces(values, direction):
    inverse = 1.0 / values[0]
    speeds = [values[1 + d] * inverse for d in range(3)]
    pressure = 0.4 * (
        values[4] - 0.5 * (values[1] * speeds[0] + values[2] * speeds[1] + values[3] * speeds[2])
    )
    velocity = speeds[direction]
    pieces = [values[1 + direction]]
    for component in range(1, 4):
        moment = values[component] * velocity
        if component - 1 == direction:
            moment = moment + pressure
        pieces.append(moment)
    pieces.append((values[4] + pressure) * velocity)
    return pieces


def matmul(a, b):
    return jnp.dot(a, b, precision=highest, preferred_element_type=jnp.float32)


def wall_kernel(count, fields, place_ref, own_ref, *refs):
    received = refs[: count - 1]
    matrix_ref = refs[count - 1]
    outs = refs[count:]
    rows, cells = own_ref.shape[2:]
    sources = [own_ref] + list(received)
    lines = []
    for source in sources:
        lines.append(
            jnp.concatenate(flux_pieces([source[f, 0] for f in range(fields)], 1), axis=1)
        )
    term = matmul(matrix_ref[...], jnp.concatenate(lines, axis=0))
    for s, out in enumerate(outs):
        for f in range(fields):
            out[f, 0] = term[s * rows : (s + 1) * rows, f * cells : (f + 1) * cells]


def wall_part(place, conserved, received, matrix, offset, part):
    fields, span, rows, cells = conserved.shape
    count = len(received) + 1
    group = span // count
    block = (fields, 1, rows, cells)
    piece = pl.BlockSpec(block, lambda i, place: (0, i, 0, 0))
    within = lambda a: piece if a.shape[1] == part else whole
    whole = pl.BlockSpec(block, lambda i, place: (0, offset + i, 0, 0))
    return pl.pallas_call(
        functools.partial(wall_kernel, count, fields),
        out_shape=[jax.ShapeDtypeStruct((fields, part, rows, cells), jnp.float32)] * count,
        grid_spec=pltpu.PrefetchScalarGridSpec(
            num_scalar_prefetch=1,
            grid=(part,),
            in_specs=[pl.BlockSpec(block, lambda i, place: (0, place[0] * group + offset + i, 0, 0))]
            + [within(a) for a in received]
            + [pl.BlockSpec(matrix.shape, lambda i, place: (0, 0))],
            out_specs=[piece] * count,
        ),
        compiler_params=pltpu.CompilerParams(vmem_limit_bytes=vmem_limit),
        cost_estimate=small_cost,
        name="wall_part",
    )(place, conserved, *received, matrix)


def inlet_kernel(table_ref, source_ref, gain_ref, out_ref, split):
    slots, fields, lines, lanes = table_ref.shape
    height = slots * lines

    @pl.when(pl.program_id(0) == 0)
    def _():
        for f in range(fields):
            rest = table_ref[:, f].reshape(height, lanes)
            for k in range(3):
                piece = rest.astype(jnp.bfloat16)
                split[pl.ds((k * fields + f) * lanes, lanes), :] = piece.T
                rest = rest - piece.astype(jnp.float32)

    width = source_ref.shape[1]
    source = source_ref[...]
    line = source // lanes
    choice = jnp.where(
        lax.broadcasted_iota(jnp.int32, (height, width), 0) == line, 1.0, 0.0
    ).astype(jnp.bfloat16)
    lane = lax.broadcasted_iota(jnp.int32, (lanes, width), 0) == source % lanes
    found = jnp.dot(split[...], choice, preferred_element_type=jnp.float32)
    found = found.reshape(3, fields, lanes, width)
    for f in range(fields):
        total = found[2, f] + found[1, f] + found[0, f]
        picked = jnp.sum(jnp.where(lane, total, 0.0), axis=0, keepdims=True)
        picked = picked * gain_ref[f]
        for k in range(width // lanes):
            out_ref[f, k : k + 1, :] = picked[:, k * lanes : (k + 1) * lanes]


def inlet_part(table, source, gain):
    slots, fields, lines, lanes = table.shape
    height = slots * lines
    columns = source.shape[1]
    width = 8 * lanes
    row = pl.BlockSpec((1, width), lambda i: (0, i))
    return pl.pallas_call(
        inlet_kernel,
        out_shape=jax.ShapeDtypeStruct((fields, columns // lanes, lanes), jnp.float32),
        grid=(columns // width,),
        in_specs=[
            pl.BlockSpec(table.shape, lambda i: (0, 0, 0, 0)),
            row,
            pl.BlockSpec(memory_space=pltpu.SMEM),
        ],
        out_specs=pl.BlockSpec((fields, 8, lanes), lambda i: (0, i, 0)),
        scratch_shapes=[pltpu.VMEM((3 * fields * lanes, height), jnp.bfloat16)],
        compiler_params=pltpu.CompilerParams(vmem_limit_bytes=vmem_limit),
        cost_estimate=small_cost,
        name="inlet_part",
    )(table, source, gain)


def local_kernel(
    halo,
    cons_ref,
    before_ref,
    after_ref,
    reg_ref,
    inlet_ref,
    near_ref,
    far_ref,
    matrix_ref,
    band_ref,
    stream_ref,
    current_ref,
    partial_ref,
    span_flux,
    stream_flux,
    span_out,
):
    fields, span, tile, cells = cons_ref.shape
    wide = span + 2 * halo
    lane = lax.broadcasted_iota(jnp.int32, (tile, cells), 1)
    for z in range(wide):
        if z < halo:
            source, at = before_ref, z
        elif z < halo + span:
            source, at = cons_ref, z - halo
        else:
            source, at = after_ref, z - halo - span
        values = [
            jnp.where(lane == 0, inlet_ref[f, :, z : z + 1], source[f, at]) for f in range(fields)
        ]
        for f, piece in enumerate(flux_pieces(values, 2)):
            for t in range(cells // 128):
                span_flux[t, pl.ds((f * wide + z) * tile, tile), :] = piece[:, t * 128 : t * 128 + 128]
        if source is cons_ref:
            for f, piece in enumerate(flux_pieces(values, 0)):
                stream_flux[pl.ds((f * span + at) * tile, tile), :] = piece
                current_ref[f, at] = values[f]
    band = band_ref[...]
    for f in range(fields):
        for y in range(tile):
            for t in range(cells // 128):
                lines = span_flux[t, pl.ds(f * wide * tile + y, wide, stride=tile), :]
                span_out[t, pl.ds(f * span * tile + y, span, stride=tile), :] = matmul(band, lines)
    lines = near_ref.shape[1]
    near = flux_pieces([near_ref[f] for f in range(fields)], 1)
    far = flux_pieces([far_ref[f] for f in range(fields)], 1)
    folds = 128 // span
    height = far_ref.shape[1]
    edges = []
    for f in range(fields):
        edge = matmul(matrix_ref[:, :lines], near[f])[:, halo : halo + span]
        for h in range(folds):
            low = lines + h * height
            part = matmul(matrix_ref[:, low : low + height], far[f])
            edge = edge + part[:, h * span : (h + 1) * span]
        edges.append(edge)
    weights = stream_ref[...]
    for f in range(fields):
        rows = pl.ds(f * span * tile, span * tile)
        beside = jnp.concatenate([span_out[t, rows, :] for t in range(cells // 128)], axis=1)
        total = matmul(stream_flux[rows, :], weights) + beside
        total = total.reshape(span, tile, cells)
        for z in range(span):
            term = total[z] + jnp.where(lane == 0, edges[f][:, z : z + 1], 0.0)
            partial_ref[f, z] = section_decay * reg_ref[f, z] - time_step * term


def local_part(conserved, before, after, register, near, far, matrix, band, weights):
    fields, span, rows, cells = conserved.shape
    halo = before.shape[1]
    wide = span + 2 * halo
    tile = 8
    main = pl.BlockSpec((fields, span, tile, cells), lambda i: (0, 0, i, 0))
    side = pl.BlockSpec((fields, halo, tile, cells), lambda i: (0, 0, i, 0))
    whole = lambda a: pl.BlockSpec(a.shape, lambda i: (0, 0))
    whole3 = lambda a: pl.BlockSpec(a.shape, lambda i: (0, 0, 0))
    shape = jax.ShapeDtypeStruct(conserved.shape, jnp.float32)
    return pl.pallas_call(
        functools.partial(local_kernel, halo),
        out_shape=[shape, shape],
        grid=(rows // tile,),
        in_specs=[
            main,
            side,
            side,
            main,
            pl.BlockSpec((fields, tile, near.shape[2]), lambda i: (0, i, 0)),
            whole3(near),
            whole3(far),
            pl.BlockSpec((tile, matrix.shape[1]), lambda i: (i, 0)),
            whole(band),
            whole(weights),
        ],
        out_specs=[main, main],
        scratch_shapes=[
            pltpu.VMEM((cells // 128, fields * wide * tile + tile, 128), jnp.float32),
            pltpu.VMEM((fields * span * tile, cells), jnp.float32),
            pltpu.VMEM((cells // 128, fields * span * tile + tile, 128), jnp.float32),
        ],
        compiler_params=pltpu.CompilerParams(vmem_limit_bytes=vmem_limit),
        cost_estimate=small_cost,
        name="local_part",
    )(conserved, before, after, register, near, near, far, matrix, band, weights)


def close_kernel(place_ref, current_ref, partial_ref, term_ref, cons_out, reg_out):
    lane = lax.broadcasted_iota(jnp.int32, term_ref.shape, 3)
    new = partial_ref[...] - time_step * jnp.where(lane == 0, 0.0, term_ref[...])
    reg_out[...] = new
    cons_out[...] = current_ref[...] + section_gain * new


def close_part(place, current, partial, term, group, offset):
    fields, part, rows, cells = term.shape
    step = math.gcd(math.gcd(part, 2), math.gcd(group, offset))
    block = (fields, step, rows, cells)
    there = pl.BlockSpec(
        block, lambda i, place: (0, (place[0] * group + offset) // step + i, 0, 0)
    )
    shape = jax.ShapeDtypeStruct(current.shape, jnp.float32)
    return pl.pallas_call(
        close_kernel,
        out_shape=[shape, shape],
        grid_spec=pltpu.PrefetchScalarGridSpec(
            num_scalar_prefetch=1,
            grid=(part // step,),
            in_specs=[there, there, pl.BlockSpec(block, lambda i, place: (0, i, 0, 0))],
            out_specs=[there, there],
        ),
        input_output_aliases={1: 0, 2: 1},
        compiler_params=pltpu.CompilerParams(vmem_limit_bytes=vmem_limit),
        cost_estimate=small_cost,
        name="close_part",
    )(place, current, partial, term)


def stream_weights(blocks):
    count, _, width, _ = blocks.shape
    lines = []
    for k in range(count):
        empty = jnp.zeros((width, width), jnp.float32)
        near = [blocks[i, 1 + k - i].T if abs(k - i) <= 1 else empty for i in range(count)]
        lines.append(jnp.concatenate(near, axis=1))
    return jnp.concatenate(lines, axis=0)


def span_band(blocks):
    count, _, width, _ = blocks.shape
    lines = []
    for k in range(count):
        line = [jnp.zeros((width, k * width), jnp.float32)] if k else []
        line += [blocks[k, j] for j in range(3)]
        line += [jnp.zeros((width, (count - 1 - k) * width), jnp.float32)] if k < count - 1 else []
        lines.append(jnp.concatenate(line, axis=1))
    return jnp.concatenate(lines, axis=0)


def local(
    conserved,
    register,
    stream_blocks,
    wall_matrix,
    span_blocks,
    inflow_gain,
    source_block,
    source_column,
):
    fields, span, rows, cells = conserved.shape
    columns = span * rows
    count = lax.axis_size("py")
    across = lax.axis_size("pz")
    row = lax.axis_index("py")
    group = span // count
    sizes = [group - group // 2, group // 2] if group >= 2 else [group]
    offsets = [sum(sizes[:c]) for c in range(len(sizes))]
    width = span_blocks.shape[2]
    steps = order_of_steps(count)
    place = lambda s: jnp.reshape((row + s) % count, (1,)).astype(jnp.int32)

    def outgoing(source, s, offset, length):
        start = ((row - s) % count) * group + offset
        return lax.dynamic_slice_in_dim(source, start, length, 1)

    received = [{} for _ in sizes]
    sent = [outgoing(conserved, steps[-1], 0, sizes[0])]
    received[0][steps[-1]] = shift(sent[0], "py", -steps[-1])
    for s in steps[:-1]:
        sent.append(outgoing(after(conserved, *sent), s, 0, group))
        arrived = shift(sent[-1], "py", -s)
        for part in received:
            part[s] = arrived
    for c in range(1, len(sizes)):
        sent.append(outgoing(after(conserved, *sent), steps[-1], offsets[c], sizes[c]))
        piece = after(sent[-1], received[0][steps[0]])
        received[c][steps[-1]] = shift(piece, "py", -steps[-1])
    head, tail = after((conserved[:, :width], conserved[:, span - width :]), *sent)
    halo_after = shift(head, "pz", -1)
    halo_before = shift(tail, "pz", 1)

    place_of = lambda a: lax.dynamic_index_in_dim(
        a.reshape(count, across, columns), lax.axis_index("pz"), 1, keepdims=False
    )
    beside = lambda a, step: lax.dynamic_index_in_dim(
        lax.dynamic_index_in_dim(a.reshape(count, across, columns), row, 0, keepdims=False),
        (lax.axis_index("pz") + step) % across,
        0,
        keepdims=False,
    )
    edge_columns = width * rows

    def sources(a):
        lines = place_of(a)
        lines = lax.dynamic_slice_in_dim(jnp.concatenate([lines, lines]), row, count, 0)
        near = jnp.concatenate(
            [beside(a, -1)[columns - edge_columns :], lines[0], beside(a, 1)[:edge_columns]]
        )
        near = near.reshape(-1, rows).T
        near = jnp.pad(near, ((0, 0), (0, 128 - near.shape[1])))
        far = lines[1:].reshape(count - 1, span, rows).swapaxes(1, 2)
        far = far.reshape(128 // span, -1, span).swapaxes(0, 1)
        return near.reshape(1, -1), far.reshape(1, -1)

    block = source_block[:, :, 0]
    near_source, far_source = sources(
        ((block % across) * count + block // across) * columns + source_column
    )

    twice = jnp.concatenate([wall_matrix, wall_matrix], axis=0)
    twice = lax.dynamic_slice_in_dim(twice, row * rows, count * rows, 0)
    twice = jnp.concatenate([twice, twice], axis=1)
    matrix = lax.dynamic_slice_in_dim(twice, row * rows, count * rows, 1)

    local_blocks = span // width
    own_blocks = lax.dynamic_slice_in_dim(
        span_blocks, lax.axis_index("pz") * local_blocks, local_blocks, 0
    )
    band = span_band(own_blocks)
    weights = stream_weights(stream_blocks)
    small = [matrix, band, weights, near_source, far_source]

    recycle = after(conserved, head, tail, *small)[:, :, :, 3 * cells // 4].reshape(-1, 128)
    along = lax.all_to_all(
        jnp.broadcast_to(recycle, (count,) + recycle.shape), "py", split_axis=0, concat_axis=0
    )

    along = after(along, *received[0].values())
    prepared = [band, weights, near_source, far_source, halo_after, halo_before]

    def wall(c, *earlier):
        return wall_part(
            place(0),
            conserved,
            [received[c][s] for s in range(1, count)],
            after(matrix, *earlier),
            offsets[c],
            sizes[c],
        )

    returned = [{} for _ in sizes]

    def give(c, pieces, *earlier):
        returned[c][0] = pieces[0]
        for s in steps:
            returned[c][s] = shift(after(pieces[s], *earlier), "py", s)

    walls = [wall(0, *prepared)]
    give(0, walls[0])

    table = lax.all_gather(along, "pz", axis=0).reshape(across * count, fields, -1, 128)
    near = inlet_part(table, after(near_source, walls[0][0]), inflow_gain)
    far = inlet_part(table, after(far_source, near), inflow_gain)
    current, partial = local_part(
        conserved,
        halo_before,
        halo_after,
        register,
        near,
        far,
        matrix,
        band,
        weights,
    )
    for c in range(1, len(sizes)):
        walls.append(wall(c, far))
        give(c, walls[c])
    for c in range(len(sizes)):
        for s in [0] + steps:
            current, partial = close_part(
                place(-s), current, partial, returned[c][s], group, offsets[c]
            )
    return (current, partial)


def solution(mesh):
    return jax.shard_map(
        local,
        mesh=mesh,
        in_specs=(
            P(None, "pz", "py", None),
            P(None, "pz", "py", None),
            P(),
            P(),
            P(),
            P(),
            P(),
            P(),
        ),
        out_specs=(P(None, "pz", "py", None), P(None, "pz", "py", None)),
        check_vma=False,
    )
```
